256 devices in a mesh: replica: 32 (over y, x, core), tensor: 8 (over z).
Axes of the slice: x: 4, y: 4, z: 8, core: 2. Of those that a mesh axis runs over, the one named last changes fastest.
Arguments:
- gate_grad: bfloat16 [32, 3072, 1024], P('replica', 'tensor'), may hold values from -16 to 16
- up_grad: bfloat16 [32, 3072, 1024], P('replica', 'tensor'), may hold values from -16 to 16
- down_grad: bfloat16 [32, 1024, 3072], P('replica', None, 'tensor'), may hold values from -16 to 16
- gate_error: bfloat16 [32, 3072, 1024], P('replica', 'tensor'), may hold values from -6 to 6
- up_error: bfloat16 [32, 3072, 1024], P('replica', 'tensor'), may hold values from -6 to 6
- down_error: bfloat16 [32, 1024, 3072], P('replica', None, 'tensor'), may hold values from -6 to 6
- q_init: float32 [3, 1024, 32], replicated, may hold values from -6 to 6
Outputs:
- gate_update: bfloat16 [3072, 1024], P('tensor')
- up_update: bfloat16 [3072, 1024], P('tensor')
- down_update: bfloat16 [1024, 3072], P(None, 'tensor')
- gate_error_next: bfloat16 [32, 3072, 1024], P('replica', 'tensor')
- up_error_next: bfloat16 [32, 3072, 1024], P('replica', 'tensor')
- down_error_next: bfloat16 [32, 1024, 3072], P('replica', None, 'tensor')
- q_next: float32 [3, 1024, 32], replicated
The draws below stay inside these ranges and needn't reach their ends.
All inputs are finite; a program needn't handle non-finite values.
Results may differ from the reference program's by a relative error of at most 0.0015.
Values sent between devices are 32-bit elements; how exact they have to be, the bound alone decides.
A program may use at most 64 MiB of HBM per device.

```python
import jax
import jax.numpy as jnp
from jax import lax

D = 1024
FF = 3072
RANK = 32
ITERS = 2
REPLICAS = 32


def grad_law(key, rows, cols, common_scale, row_low):
    key_common, key_noise, key_rows = jax.random.split(key, 3)
    common = jnp.clip(jax.random.normal(key_common, (rows, cols), jnp.float32), -4.0, 4.0) * common_scale
    noise = jnp.clip(jax.random.normal(key_noise, (REPLICAS, rows, cols), jnp.float32), -4.0, 4.0)
    row_gain = jnp.exp(jax.random.uniform(key_rows, (1, rows, 1), jnp.float32, jnp.log(row_low), 0.0))
    return ((common[None] + noise) * row_gain).astype(jnp.bfloat16)


def draw_gate_grad(key, part):
    key = jax.random.fold_in(key, 11)
    return grad_law(key, FF, D, 3.0, 1.0)


def draw_up_grad(key, part):
    key = jax.random.fold_in(key, 12)
    return grad_law(key, FF, D, 3.0, 1.0)


def draw_down_grad(key, part):
    key = jax.random.fold_in(key, 13)
    return grad_law(key, D, FF, 3.0, 1.0)


def level_of(key, extent, cuts, least, top_value):
    def one(position, parts):
        steps = jax.random.uniform(jax.random.fold_in(jax.random.fold_in(key, 6), position), (parts,), jnp.float32, least / len(cuts), top_value / len(cuts))
        return jnp.repeat(jnp.exp(steps), extent[position] // parts).reshape((-1,) + (1,) * (len(extent) - position - 1))

    factor_of = one(*cuts[0])
    for cut in cuts[1:]:
        factor_of = factor_of * one(*cut)
    return factor_of


def bell_draw(rng, shape, scale, limit, cuts=(), kind=jnp.bfloat16):
    gain = level_of(rng, shape, cuts, -0.22, 0.18) if cuts else 1.0
    drawn = jax.random.normal(rng, shape, jnp.float32) * scale * gain
    return jnp.minimum(jnp.maximum(drawn, -limit), limit).astype(kind)


def setup_inputs(seed: int = 0) -> dict:
    key_of = jax.random.split(jax.random.key(seed), 8)
    gate_grad = draw_gate_grad(jax.random.fold_in(key_of[7], 71), 0)
    up_grad = draw_up_grad(jax.random.fold_in(key_of[7], 71), 0)
    down_grad = draw_down_grad(jax.random.fold_in(key_of[7], 71), 0)
    gate_error = bell_draw(key_of[3], (REPLICAS, FF, D), 1.0, 6.0, ((0, 32), (1, 8)))
    up_error = bell_draw(key_of[4], (REPLICAS, FF, D), 1.0, 6.0, ((0, 32), (1, 8)))
    down_error = bell_draw(key_of[5], (REPLICAS, D, FF), 1.0, 6.0, ((0, 32), (2, 8)))
    q_init = bell_draw(key_of[6], (3, D, RANK), 1.0, 6.0, (), jnp.float32)
    return {"gate_grad": gate_grad, "up_grad": up_grad, "down_grad": down_grad, "gate_error": gate_error, "up_error": up_error, "down_error": down_error, "q_init": q_init}


HI = lax.Precision.HIGHEST

def orthonormal(pmat):
    gram = jnp.dot(pmat.T.astype(jnp.float32), pmat.astype(jnp.float32), precision=HI, preferred_element_type=jnp.float32)
    lower = jnp.linalg.cholesky(gram)
    return lax.linalg.triangular_solve(lower, pmat, left_side=False, lower=True, transpose_a=True)

def compress(matrix, q_start):
    q_now = q_start
    for step in range(ITERS):
        pmat = jnp.einsum('afd,dk->fk', matrix, q_now, precision=HI) / REPLICAS
        p_hat = orthonormal(pmat)
        q_now = jnp.einsum('afd,fk->dk', matrix, p_hat, precision=HI) / REPLICAS
    update = jnp.dot(p_hat.astype(jnp.float32), q_now.T.astype(jnp.float32), precision=HI, preferred_element_type=jnp.float32)
    error_next = (matrix - update[None]).astype(jnp.bfloat16)
    return (update.astype(jnp.bfloat16), error_next, q_now)

def reference(gate_grad, up_grad, down_grad, gate_error, up_error, down_error, q_init):
    gate_m = gate_grad.astype(jnp.float32) + gate_error.astype(jnp.float32)
    gate_u, gate_e, gate_q = compress(gate_m, q_init[0])
    up_m = up_grad.astype(jnp.float32) + up_error.astype(jnp.float32)
    up_u, up_e, up_q = compress(up_m, q_init[1])
    down_m = jnp.swapaxes(down_grad.astype(jnp.float32) + down_error.astype(jnp.float32), 1, 2)
    down_u, down_e, down_q = compress(down_m, q_init[2])
    return (gate_u, up_u, down_u.T, gate_e, up_e, jnp.swapaxes(down_e, 1, 2), jnp.stack([gate_q, up_q, down_q]))
```

```python
import jax
import jax.numpy as jnp
from jax import lax
from jax.experimental import pallas as pl
from jax.experimental.pallas import tpu as pltpu
from jax.sharding import PartitionSpec as P

ITERS = 2
D = 1024
RANK = 32
ROWS = 384
NY, NX, NZ = 4, 4, 8
MESH = pl.DeviceIdType.MESH
F32 = jnp.float32
BF16 = jnp.bfloat16
PARTS = 2

P_CORE, P_ONE, P_TWO, P_BACK, GRAM, Q_CORE, Q_SCATTER, Q_Z, Q_GATHER, Q_BACK = range(10)


def split(x, parts):
    out = []
    for k in range(parts):
        piece = x.astype(BF16)
        out.append(piece)
        if k + 1 < parts:
            x = x - piece.astype(F32)
    return out


def dot(a, b, ca, cb):
    return lax.dot_general(a, b, (((ca,), (cb,)), ((), ())), preferred_element_type=F32)


def small_left(a, cat_axis):
    h, m, l = split(a, 3)
    return jnp.concatenate([h, h, m, h, l, m], axis=cat_axis)


def small_right(b):
    h, m, l = split(b, 3)
    return jnp.concatenate([h, m, h, l, h, m], axis=0)


def fold(x, parts):
    total = x[(parts - 1) * RANK :]
    for k in range(parts - 2, -1, -1):
        total = total + x[k * RANK : (k + 1) * RANK]
    return total


def inverse_factors(grams):
    row = lax.broadcasted_iota(jnp.int32, (RANK, 2 * RANK), 0)
    lane = lax.broadcasted_iota(jnp.int32, (RANK, 2 * RANK), 1)
    eye = (lane == row + RANK).astype(F32)
    augs = []
    for g in grams:
        augs.append(jnp.concatenate([g, jnp.zeros_like(g)], axis=1) + eye)
    for j in range(RANK):
        for n in range(len(augs)):
            a = augs[n]
            pivot = a[j : j + 1, j : j + 1]
            r = lax.rsqrt(pivot)
            r = r * (1.5 - 0.5 * pivot * r * r)
            top = a[j : j + 1, :] * r
            col = a[:, j : j + 1] * r
            a = jnp.where(row > j, a - col * top, jnp.where(row == j, top, a))
            augs[n] = a
    return [a[:, RANK:] for a in augs]


def kernel(
    g0, g1, g2, e0, e1, e2, q0,
    q_out, ps_out, qs_out,
    gm, em, gd, ed, qs, pt, pc, x1, x2, pf, gz, qp, qc, qsum, qr, zq, qf, linv,
    load, ssem, rsem,
):
    r = lax.axis_index("replica")
    z = lax.axis_index("tensor")
    y, x, c = r // 8, (r // 2) % 4, r % 2
    p = y * 4 + x
    other = 1 - c
    sib = (y * 8 + x * 2 + other, z)

    def at(yy, xx):
        return (yy * 8 + xx * 2 + c, z)

    plane = [
        ((y + dy) % NY, (x + dx) % NX)
        for dy, dx in [
            (2, 2), (2, 1), (1, 2), (2, 3), (3, 2), (1, 1), (1, 3), (3, 1), (3, 3),
            (2, 0), (0, 2), (1, 0), (0, 1), (3, 0), (0, 3),
        ]
    ]
    column = [(r, (z + dz) % NZ) for dz in (4, 3, 5, 2, 6, 1, 7)]
    xs = [at(y, (x + d) % NX) for d in (2, 1, 3)]
    ys = [at((y + d) % NY, x) for d in (2, 1, 3)]

    barrier = pltpu.get_barrier_semaphore()
    greet = [at(yy, xx) for yy, xx in plane] + column + [sib]
    for dev in greet:
        pl.semaphore_signal(barrier, inc=1, device_id=dev, device_id_type=MESH)

    loads = []
    for i, (src, dst) in enumerate(
        [(g0, gm.at[0]), (e0, em.at[0]), (g1, gm.at[1]), (e1, em.at[1]), (g2, gd), (e2, ed)]
    ):
        cp = pltpu.make_async_copy(src, dst, load.at[i])
        cp.start()
        loads.append(cp)

    def send(stage, t, i, src, dst, dev):
        pltpu.make_async_remote_copy(
            src_ref=src,
            dst_ref=dst,
            send_sem=ssem.at[stage, t],
            recv_sem=rsem.at[stage, t, i],
            device_id=dev,
            device_id_type=MESH,
        ).start()

    def arrived(stage, t, i, like):
        pltpu.make_async_copy(like, like, rsem.at[stage, t, i]).wait()

    for i in range(3):
        qs[i] = jnp.concatenate(split(q0[i], PARTS), axis=0)

    def project(i):
        if i == 2:
            v = dot(qs[i], gd[...], 1, 0) + dot(qs[i], ed[...], 1, 0)
        else:
            v = dot(qs[i], gm[i], 1, 1) + dot(qs[i], em[i], 1, 1)
        return fold(v, PARTS) * (1.0 / 32.0)

    def back_project(i, ps):
        if i == 2:
            v = dot(ps, gd[...], 1, 1) + dot(ps, ed[...], 1, 1)
        else:
            v = dot(ps, gm[i], 1, 0) + dot(ps, em[i], 1, 0)
        return fold(v, PARTS) * (1.0 / 32.0)

    def iteration(t, first):
        for i in range(3):
            if first:
                loads[2 * i].wait()
                loads[2 * i + 1].wait()
            pt[t, i] = project(i).reshape(4, 8, ROWS)
            if first and i == 0:
                pl.semaphore_wait(barrier, len(greet))
            send(P_CORE, t, i, pt.at[t, i, pl.ds(2 * other, 2)], pc.at[t, i], sib)
        for i in range(3):
            arrived(P_CORE, t, i, pc.at[t, i])
            s = pt[t, i, pl.ds(2 * c, 2)] + pc[t, i]
            x1[t, i, 0, x] = s[0]
            x1[t, i, 1, y] = s[1]
            for dev in xs:
                send(P_ONE, t, i, x1.at[t, i, 0, x], x1.at[t, i, 0, x], dev)
            for dev in ys:
                send(P_ONE, t, i, x1.at[t, i, 1, y], x1.at[t, i, 1, y], dev)
        for i in range(3):
            arrived(P_ONE, t, i, x1.at[t, i, :, pl.ds(0, 3)])
            a = (x1[t, i, 0, 0] + x1[t, i, 0, 1]) + (x1[t, i, 0, 2] + x1[t, i, 0, 3])
            b = (x1[t, i, 1, 0] + x1[t, i, 1, 1]) + (x1[t, i, 1, 2] + x1[t, i, 1, 3])
            x2[t, i, 0, y] = a
            x2[t, i, 1, x] = b
            for dev in ys:
                send(P_TWO, t, i, x2.at[t, i, 0, y], x2.at[t, i, 0, y], dev)
            for dev in xs:
                send(P_TWO, t, i, x2.at[t, i, 1, x], x2.at[t, i, 1, x], dev)
        for i in range(3):
            arrived(P_TWO, t, i, x2.at[t, i, :, pl.ds(0, 3)])
            a = (x2[t, i, 0, 0] + x2[t, i, 0, 1]) + (x2[t, i, 0, 2] + x2[t, i, 0, 3])
            b = (x2[t, i, 1, 0] + x2[t, i, 1, 1]) + (x2[t, i, 1, 2] + x2[t, i, 1, 3])
            pf[t, i, 2 * c] = a
            pf[t, i, 2 * c + 1] = b
            send(P_BACK, t, i, pf.at[t, i, pl.ds(2 * c, 2)], pf.at[t, i, pl.ds(2 * c, 2)], sib)
        grams = []
        for i in range(3):
            arrived(P_BACK, t, i, pf.at[t, i, pl.ds(0, 2)])
            ps = jnp.concatenate(split(pf[t, i].reshape(RANK, ROWS), PARTS), axis=0)
            term = back_project(i, ps)
            qp[t, i] = term.reshape(2, 2, 8, D)
            send(Q_CORE, t, i, qp.at[t, i, other], qc.at[t, i], sib)
            gg = fold(dot(ps, ps, 1, 1), PARTS)
            gram = gg[:, (PARTS - 1) * RANK :]
            for k in range(PARTS - 2, -1, -1):
                gram = gram + gg[:, k * RANK : (k + 1) * RANK]
            grams.append(gram)
        gz[t, z] = jnp.concatenate(grams + [jnp.zeros((RANK, RANK), F32)], axis=1)
        for dev in column:
            send(GRAM, t, 0, gz.at[t, z], gz.at[t, z], dev)
        for i in range(3):
            arrived(Q_CORE, t, i, qc.at[t, i])
            s = qp[t, i, c] + qc[t, i]
            for k in range(16):
                qsum[t, i, k] = s[k // 8, :, (k % 8) * 128 : (k % 8 + 1) * 128]
            qr[t, i, p] = qsum[t, i, p]
            for yy, xx in plane:
                send(Q_SCATTER, t, i, qsum.at[t, i, yy * 4 + xx], qr.at[t, i, p], at(yy, xx))
        for i in range(3):
            arrived(Q_SCATTER, t, i, qr.at[t, i, pl.ds(0, 15)])
            zq[t, i, z] = jnp.sum(qr[t, i], axis=0)
            for dev in column:
                send(Q_Z, t, i, zq.at[t, i, z], zq.at[t, i, z], dev)
        arrived(GRAM, t, 0, gz.at[t, pl.ds(0, 7)])
        gram = jnp.sum(gz[t], axis=0)
        inv = inverse_factors([gram[:, k * RANK : (k + 1) * RANK] for k in range(3)])
        for i in range(3):
            linv[i] = small_left(inv[i], 1)
        for i in range(3):
            arrived(Q_Z, t, i, zq.at[t, i, pl.ds(0, 7)])
            qf[t, i, c, p] = jnp.sum(zq[t, i], axis=0)
            for yy, xx in plane:
                send(Q_GATHER, t, i, qf.at[t, i, c, p], qf.at[t, i, c, p], at(yy, xx))
        for i in range(3):
            arrived(Q_GATHER, t, i, qf.at[t, i, 0, pl.ds(0, 15)])
            send(Q_BACK, t, i, qf.at[t, i, c], qf.at[t, i, c], sib)
        for i in range(3):
            arrived(Q_BACK, t, i, qf.at[t, i, 0])
            full = qf[t, i]
            raw = jnp.concatenate(
                [
                    jnp.concatenate([full[k // 2, (k % 2) * 8 + l] for l in range(8)], axis=1)
                    for k in range(4)
                ],
                axis=0,
            )
            q_now = dot(linv[i], small_right(raw), 1, 0)
            if first:
                qs[i] = jnp.concatenate(split(q_now, PARTS), axis=0)
            else:
                q_out[i] = q_now
                qh, ql = split(q_now, 2)
                qs_out[i] = jnp.concatenate([qh, ql, qh], axis=0)
                p_hat = dot(linv[i], small_right(pf[t, i].reshape(RANK, ROWS)), 1, 0)
                ph, pw = split(p_hat, 2)
                ps_out[i] = jnp.concatenate([ph, ph, pw], axis=0)

    for t in range(ITERS):
        iteration(t, t == 0)

    def sent(stage, t, like):
        pltpu.make_async_copy(like, like, ssem.at[stage, t]).wait()

    for t in range(ITERS):
        sent(P_CORE, t, pc.at[t])
        sent(P_ONE, t, x1.at[t, :, :, pl.ds(0, 3)])
        sent(P_TWO, t, x2.at[t, :, :, pl.ds(0, 3)])
        sent(P_BACK, t, pf.at[t, :, pl.ds(0, 2)])
        sent(GRAM, t, gz.at[t, pl.ds(0, 7)])
        sent(Q_CORE, t, qc.at[t])
        sent(Q_SCATTER, t, qr.at[t, :, pl.ds(0, 15)])
        sent(Q_Z, t, zq.at[t, :, pl.ds(0, 7)])
        sent(Q_GATHER, t, qf.at[t, :, 0, pl.ds(0, 15)])
        sent(Q_BACK, t, qf.at[t, :, 0])


def exchange(grads, errors, q0):
    vmem = lambda *shape: pltpu.VMEM(shape, F32)
    scratch = [
        pltpu.VMEM((2, ROWS, D), BF16),
        pltpu.VMEM((2, ROWS, D), BF16),
        pltpu.VMEM((D, ROWS), BF16),
        pltpu.VMEM((D, ROWS), BF16),
        pltpu.VMEM((3, PARTS * RANK, D), BF16),
        vmem(ITERS, 3, 4, 8, ROWS),
        vmem(ITERS, 3, 2, 8, ROWS),
        vmem(ITERS, 3, 2, 4, 8, ROWS),
        vmem(ITERS, 3, 2, 4, 8, ROWS),
        vmem(ITERS, 3, 4, 8, ROWS),
        vmem(ITERS, NZ, RANK, 128),
        vmem(ITERS, 3, 2, 2, 8, D),
        vmem(ITERS, 3, 2, 8, D),
        vmem(ITERS, 3, 16, 8, 128),
        vmem(ITERS, 3, 16, 8, 128),
        vmem(ITERS, 3, NZ, 8, 128),
        vmem(ITERS, 3, 2, 16, 8, 128),
        pltpu.VMEM((3, RANK, 6 * RANK), BF16),
        pltpu.SemaphoreType.DMA((6,)),
        pltpu.SemaphoreType.DMA((10, ITERS)),
        pltpu.SemaphoreType.DMA((10, ITERS, 3)),
    ]
    anywhere = pl.BlockSpec(memory_space=pl.ANY)
    inside = pl.BlockSpec(memory_space=pltpu.VMEM)
    return pl.pallas_call(
        kernel,
        name="power",
        out_shape=(
            jax.ShapeDtypeStruct((3, RANK, D), F32),
            jax.ShapeDtypeStruct((3, 3 * RANK, ROWS), BF16),
            jax.ShapeDtypeStruct((3, 3 * RANK, D), BF16),
        ),
        in_specs=[anywhere] * 6 + [inside],
        out_specs=(inside, inside, inside),
        scratch_shapes=scratch,
        compiler_params=pltpu.CompilerParams(
            collective_id=0, has_side_effects=True, vmem_limit_bytes=32 << 20
        ),
        cost_estimate=pl.CostEstimate(flops=10**9, bytes_accessed=6 * 10**6, transcendentals=0),
    )(*grads, *errors, q0)


STEPS = 4
WIDE = D // STEPS


def finish_kernel(ps, qs, q, g0, g1, g2, e0, e1, e2, u0, u1, u2, n0, n1, n2, q_out):
    def one(g, e, u, n, left, right):
        v = dot(left, right, 0, 0)
        u[...] = v.astype(BF16)
        n[...] = ((g[...].astype(F32) + e[...].astype(F32)) - v).astype(BF16)

    one(g0, e0, u0, n0, ps[0], qs[0])
    one(g1, e1, u1, n1, ps[1], qs[1])
    one(g2, e2, u2, n2, qs[2], ps[2])
    q_out[...] = q[...]


def finish(ps, qs, q, grads, errors):
    tall = pl.BlockSpec((ROWS, WIDE), lambda s: (0, s))
    flat = pl.BlockSpec((WIDE, ROWS), lambda s: (s, 0))
    q_spec = pl.BlockSpec((3, RANK, WIDE), lambda s: (0, 0, s))
    shapes = [(ROWS, D), (ROWS, D), (D, ROWS)]
    outs = [jax.ShapeDtypeStruct(shape, BF16) for shape in shapes]
    return pl.pallas_call(
        finish_kernel,
        name="finish",
        grid=(STEPS,),
        in_specs=[
            pl.BlockSpec((3, 3 * RANK, ROWS), lambda s: (0, 0, 0)),
            pl.BlockSpec((3, 3 * RANK, WIDE), lambda s: (0, 0, s)),
            q_spec,
            tall, tall, flat, tall, tall, flat,
        ],
        out_specs=[tall, tall, flat, tall, tall, flat, q_spec],
        out_shape=outs + outs + [jax.ShapeDtypeStruct((3, RANK, D), F32)],
        compiler_params=pltpu.CompilerParams(vmem_limit_bytes=32 << 20),
    )(ps, qs, q, *grads, *errors)


def shards(gate_grad, up_grad, down_grad, gate_error, up_error, down_error, q_init):
    grads = (gate_grad[0], up_grad[0], down_grad[0])
    errors = (gate_error[0], up_error[0], down_error[0])
    q, ps, qs = exchange(grads, errors, jnp.swapaxes(q_init, 1, 2))
    u0, u1, u2, n0, n1, n2, q_next = finish(ps, qs, q, grads, errors)
    return u0, u1, u2, n0[None], n1[None], n2[None], jnp.swapaxes(q_next, 1, 2)


def solution(mesh):
    in_specs = (
        P("replica", "tensor", None),
        P("replica", "tensor", None),
        P("replica", None, "tensor"),
        P("replica", "tensor", None),
        P("replica", "tensor", None),
        P("replica", None, "tensor"),
        P(),
    )
    out_specs = (
        P("tensor", None),
        P("tensor", None),
        P(None, "tensor"),
        P("replica", "tensor", None),
        P("replica", "tensor", None),
        P("replica", None, "tensor"),
        P(),
    )
    return jax.shard_map(shards, mesh=mesh, in_specs=in_specs, out_specs=out_specs, check_vma=False)
```

```python
import jax
import jax.numpy as jnp
from jax import lax
from jax.experimental import pallas as pl
from jax.experimental.pallas import tpu as pltpu
from jax.sharding import PartitionSpec as P

ITERS = 2
D = 1024
RANK = 32
ROWS = 384
NY, NX, NZ = 4, 4, 8
MESH = pl.DeviceIdType.MESH
F32 = jnp.float32
BF16 = jnp.bfloat16
PARTS = 2

P_CORE, P_ONE, P_TWO, P_BACK, GRAM, Q_CORE, Q_SCATTER, Q_Z, Q_GATHER, Q_BACK = range(10)


def split(x, parts):
    out = []
    for k in range(parts):
        piece = x.astype(BF16)
        out.append(piece)
        if k + 1 < parts:
            x = x - piece.astype(F32)
    return out


def dot(a, b, ca, cb):
    return lax.dot_general(a, b, (((ca,), (cb,)), ((), ())), preferred_element_type=F32)


def small_left(a, cat_axis):
    h, m, l = split(a, 3)
    return jnp.concatenate([h, h, m, h, l, m], axis=cat_axis)


def small_right(b):
    h, m, l = split(b, 3)
    return jnp.concatenate([h, m, h, l, h, m], axis=0)


def fold(x, parts):
    total = x[(parts - 1) * RANK :]
    for k in range(parts - 2, -1, -1):
        total = total + x[k * RANK : (k + 1) * RANK]
    return total


def inverse_factors(grams):
    row = lax.broadcasted_iota(jnp.int32, (RANK, 2 * RANK), 0)
    lane = lax.broadcasted_iota(jnp.int32, (RANK, 2 * RANK), 1)
    eye = (lane == row + RANK).astype(F32)
    augs = []
    for g in grams:
        augs.append(jnp.concatenate([g, jnp.zeros_like(g)], axis=1) + eye)
    for j in range(RANK):
        for n in range(len(augs)):
            a = augs[n]
            pivot = a[j : j + 1, j : j + 1]
            r = lax.rsqrt(pivot)
            r = r * (1.5 - 0.5 * pivot * r * r)
            top = a[j : j + 1, :] * r
            col = a[:, j : j + 1] * r
            a = jnp.where(row > j, a - col * top, jnp.where(row == j, top, a))
            augs[n] = a
    return [a[:, RANK:] for a in augs]


def kernel(
    g0, g1, g2, e0, e1, e2, q0,
    q_out, ps_out, qs_out, gm, em, gd, ed,
    qi, qs, pt, pc, x1, x2, pf, gz, qp, qc, qsum, qr, zq, qf, linv,
    load, ssem, rsem,
):
    r = lax.axis_index("replica")
    z = lax.axis_index("tensor")
    y, x, c = r // 8, (r // 2) % 4, r % 2
    p = y * 4 + x
    other = 1 - c
    sib = (y * 8 + x * 2 + other, z)

    def at(yy, xx):
        return (yy * 8 + xx * 2 + c, z)

    plane = [
        ((y + dy) % NY, (x + dx) % NX)
        for dy, dx in [
            (2, 2), (2, 1), (1, 2), (2, 3), (3, 2), (1, 1), (1, 3), (3, 1), (3, 3),
            (2, 0), (0, 2), (1, 0), (0, 1), (3, 0), (0, 3),
        ]
    ]
    column = [(r, (z + dz) % NZ) for dz in (4, 3, 5, 2, 6, 1, 7)]
    xs = [at(y, (x + d) % NX) for d in (2, 1, 3)]
    ys = [at((y + d) % NY, x) for d in (2, 1, 3)]

    barrier = pltpu.get_barrier_semaphore()
    greet = [at(yy, xx) for yy, xx in plane] + column + [sib]
    for dev in greet:
        pl.semaphore_signal(barrier, inc=1, device_id=dev, device_id_type=MESH)

    loads = []
    for i, (src, dst) in enumerate(
        [(g0, gm.at[0]), (e0, em.at[0]), (g1, gm.at[1]), (e1, em.at[1]), (g2, gd), (e2, ed), (q0, qi)]
    ):
        cp = pltpu.make_async_copy(src, dst, load.at[i])
        loads.append(cp)
    for k in (6, 0, 1, 2, 3, 4, 5):
        loads[k].start()

    def send(stage, t, i, src, dst, dev):
        pltpu.make_async_remote_copy(
            src_ref=src,
            dst_ref=dst,
            send_sem=ssem.at[stage, t],
            recv_sem=rsem.at[stage, t, i],
            device_id=dev,
            device_id_type=MESH,
        ).start()

    def arrived(stage, t, i, like):
        pltpu.make_async_copy(like, like, rsem.at[stage, t, i]).wait()

    loads[6].wait()
    for i in range(3):
        qs[i] = jnp.concatenate(split(qi[i], PARTS), axis=0)

    def project(i):
        if i == 2:
            v = dot(qs[i], gd[...], 1, 0) + dot(qs[i], ed[...], 1, 0)
        else:
            v = dot(qs[i], gm[i], 1, 1) + dot(qs[i], em[i], 1, 1)
        return fold(v, PARTS) * (1.0 / 32.0)

    def back_project(i, ps):
        if i == 2:
            v = dot(ps, gd[...], 1, 1) + dot(ps, ed[...], 1, 1)
        else:
            v = dot(ps, gm[i], 1, 0) + dot(ps, em[i], 1, 0)
        return fold(v, PARTS) * (1.0 / 32.0)

    def iteration(t, first):
        for i in range(3):
            if first:
                loads[2 * i].wait()
                loads[2 * i + 1].wait()
            pt[t, i] = project(i).reshape(4, 8, ROWS)
            if first and i == 0:
                pl.semaphore_wait(barrier, len(greet))
            send(P_CORE, t, i, pt.at[t, i, pl.ds(2 * other, 2)], pc.at[t, i], sib)
        for i in range(3):
            arrived(P_CORE, t, i, pc.at[t, i])
            s = pt[t, i, pl.ds(2 * c, 2)] + pc[t, i]
            x1[t, i, 0, x] = s[0]
            x1[t, i, 1, y] = s[1]
            for dev in xs:
                send(P_ONE, t, i, x1.at[t, i, 0, x], x1.at[t, i, 0, x], dev)
            for dev in ys:
                send(P_ONE, t, i, x1.at[t, i, 1, y], x1.at[t, i, 1, y], dev)
        for i in range(3):
            arrived(P_ONE, t, i, x1.at[t, i, :, pl.ds(0, 3)])
            a = (x1[t, i, 0, 0] + x1[t, i, 0, 1]) + (x1[t, i, 0, 2] + x1[t, i, 0, 3])
            b = (x1[t, i, 1, 0] + x1[t, i, 1, 1]) + (x1[t, i, 1, 2] + x1[t, i, 1, 3])
            x2[t, i, 0, y] = a
            x2[t, i, 1, x] = b
            for dev in ys:
                send(P_TWO, t, i, x2.at[t, i, 0, y], x2.at[t, i, 0, y], dev)
            for dev in xs:
                send(P_TWO, t, i, x2.at[t, i, 1, x], x2.at[t, i, 1, x], dev)
        for i in range(3):
            arrived(P_TWO, t, i, x2.at[t, i, :, pl.ds(0, 3)])
            a = (x2[t, i, 0, 0] + x2[t, i, 0, 1]) + (x2[t, i, 0, 2] + x2[t, i, 0, 3])
            b = (x2[t, i, 1, 0] + x2[t, i, 1, 1]) + (x2[t, i, 1, 2] + x2[t, i, 1, 3])
            pf[t, i, 2 * c] = a
            pf[t, i, 2 * c + 1] = b
            send(P_BACK, t, i, pf.at[t, i, pl.ds(2 * c, 2)], pf.at[t, i, pl.ds(2 * c, 2)], sib)
        grams = []
        for i in range(3):
            arrived(P_BACK, t, i, pf.at[t, i, pl.ds(0, 2)])
            ps = jnp.concatenate(split(pf[t, i].reshape(RANK, ROWS), PARTS), axis=0)
            term = back_project(i, ps)
            qp[t, i] = term.reshape(2, 2, 8, D)
            send(Q_CORE, t, i, qp.at[t, i, other], qc.at[t, i], sib)
            gg = fold(dot(ps, ps, 1, 1), PARTS)
            gram = gg[:, (PARTS - 1) * RANK :]
            for k in range(PARTS - 2, -1, -1):
                gram = gram + gg[:, k * RANK : (k + 1) * RANK]
            grams.append(gram)
        gz[t, z] = jnp.concatenate(grams + [jnp.zeros((RANK, RANK), F32)], axis=1)
        for dev in column:
            send(GRAM, t, 0, gz.at[t, z], gz.at[t, z], dev)
        for i in range(3):
            arrived(Q_CORE, t, i, qc.at[t, i])
            s = qp[t, i, c] + qc[t, i]
            for k in range(16):
                qsum[t, i, k] = s[k // 8, :, (k % 8) * 128 : (k % 8 + 1) * 128]
            qr[t, i, p] = qsum[t, i, p]
            for yy, xx in plane:
                send(Q_SCATTER, t, i, qsum.at[t, i, yy * 4 + xx], qr.at[t, i, p], at(yy, xx))
        for i in range(3):
            arrived(Q_SCATTER, t, i, qr.at[t, i, pl.ds(0, 15)])
            zq[t, i, z] = jnp.sum(qr[t, i], axis=0)
            for dev in column:
                send(Q_Z, t, i, zq.at[t, i, z], zq.at[t, i, z], dev)
        arrived(GRAM, t, 0, gz.at[t, pl.ds(0, 7)])
        gram = jnp.sum(gz[t], axis=0)
        inv = inverse_factors([gram[:, k * RANK : (k + 1) * RANK] for k in range(3)])
        for i in range(3):
            linv[i] = small_left(inv[i], 1)
        for i in range(3):
            arrived(Q_Z, t, i, zq.at[t, i, pl.ds(0, 7)])
            qf[t, i, c, p] = jnp.sum(zq[t, i], axis=0)
            for yy, xx in plane:
                send(Q_GATHER, t, i, qf.at[t, i, c, p], qf.at[t, i, c, p], at(yy, xx))
        for i in range(3):
            arrived(Q_GATHER, t, i, qf.at[t, i, 0, pl.ds(0, 15)])
            send(Q_BACK, t, i, qf.at[t, i, c], qf.at[t, i, c], sib)
        for i in range(3):
            arrived(Q_BACK, t, i, qf.at[t, i, 0])
            full = qf[t, i]
            raw = jnp.concatenate(
                [
                    jnp.concatenate([full[k // 2, (k % 2) * 8 + l] for l in range(8)], axis=1)
                    for k in range(4)
                ],
                axis=0,
            )
            q_now = dot(linv[i], small_right(raw), 1, 0)
            if first:
                qs[i] = jnp.concatenate(split(q_now, PARTS), axis=0)
            else:
                q_out[i] = q_now
                qh, ql = split(q_now, 2)
                qs_out[i] = jnp.concatenate([qh, ql, qh], axis=0)
                p_hat = dot(linv[i], small_right(pf[t, i].reshape(RANK, ROWS)), 1, 0)
                ph, pw = split(p_hat, 2)
                ps_out[i] = jnp.concatenate([ph, ph, pw], axis=0)

    for t in range(ITERS):
        iteration(t, t == 0)

    def sent(stage, t, like):
        pltpu.make_async_copy(like, like, ssem.at[stage, t]).wait()

    for t in range(ITERS):
        sent(P_CORE, t, pc.at[t])
        sent(P_ONE, t, x1.at[t, :, :, pl.ds(0, 3)])
        sent(P_TWO, t, x2.at[t, :, :, pl.ds(0, 3)])
        sent(P_BACK, t, pf.at[t, :, pl.ds(0, 2)])
        sent(GRAM, t, gz.at[t, pl.ds(0, 7)])
        sent(Q_CORE, t, qc.at[t])
        sent(Q_SCATTER, t, qr.at[t, :, pl.ds(0, 15)])
        sent(Q_Z, t, zq.at[t, :, pl.ds(0, 7)])
        sent(Q_GATHER, t, qf.at[t, :, 0, pl.ds(0, 15)])
        sent(Q_BACK, t, qf.at[t, :, 0])


def exchange(*operands):
    vmem = lambda *shape: pltpu.VMEM(shape, F32)
    scratch = [
        vmem(3, RANK, D),
        pltpu.VMEM((3, PARTS * RANK, D), BF16),
        vmem(ITERS, 3, 4, 8, ROWS),
        vmem(ITERS, 3, 2, 8, ROWS),
        vmem(ITERS, 3, 2, 4, 8, ROWS),
        vmem(ITERS, 3, 2, 4, 8, ROWS),
        vmem(ITERS, 3, 4, 8, ROWS),
        vmem(ITERS, NZ, RANK, 128),
        vmem(ITERS, 3, 2, 2, 8, D),
        vmem(ITERS, 3, 2, 8, D),
        vmem(ITERS, 3, 16, 8, 128),
        vmem(ITERS, 3, 16, 8, 128),
        vmem(ITERS, 3, NZ, 8, 128),
        vmem(ITERS, 3, 2, 16, 8, 128),
        pltpu.VMEM((3, RANK, 6 * RANK), BF16),
        pltpu.SemaphoreType.DMA((7,)),
        pltpu.SemaphoreType.DMA((10, ITERS)),
        pltpu.SemaphoreType.DMA((10, ITERS, 3)),
    ]
    outside = pl.BlockSpec(memory_space=pltpu.HBM)
    inside = pl.BlockSpec(memory_space=pltpu.VMEM)
    return pl.pallas_call(
        kernel,
        name="power",
        out_shape=(
            jax.ShapeDtypeStruct((3, RANK, D), F32),
            jax.ShapeDtypeStruct((3, 3 * RANK, ROWS), BF16),
            jax.ShapeDtypeStruct((3, 3 * RANK, D), BF16),
            jax.ShapeDtypeStruct((2, ROWS, D), BF16),
            jax.ShapeDtypeStruct((2, ROWS, D), BF16),
            jax.ShapeDtypeStruct((D, ROWS), BF16),
            jax.ShapeDtypeStruct((D, ROWS), BF16),
        ),
        in_specs=[outside] * 7,
        out_specs=(inside,) * 7,
        scratch_shapes=scratch,
        compiler_params=pltpu.CompilerParams(
            collective_id=0, has_side_effects=True, vmem_limit_bytes=24 << 20
        ),
        cost_estimate=pl.CostEstimate(flops=10**9, bytes_accessed=6 * 10**6, transcendentals=0),
    )(*operands)


PIECES = 4
TALL = ROWS // PIECES
FLAT = D // PIECES


def finish_kernel(ps, qs, q, gm, em, gd, ed, u0, u1, u2, n0, n1, n2, q_out, um, nm, ud, nd, sem):
    copies = []

    def out(src, dst):
        cp = pltpu.make_async_copy(src, dst, sem.at[len(copies)])
        cp.start()
        copies.append(cp)

    out(q, q_out)
    for i, (u, n) in enumerate(((u0, n0), (u1, n1))):
        for k in range(PIECES):
            rows = pl.ds(k * TALL, TALL)
            v = dot(ps[i, :, k * TALL : (k + 1) * TALL], qs[i], 0, 0)
            um[i, rows] = v.astype(BF16)
            nm[i, rows] = ((gm[i, rows].astype(F32) + em[i, rows].astype(F32)) - v).astype(BF16)
            out(um.at[i, rows], u.at[rows])
            out(nm.at[i, rows], n.at[rows])
    for k in range(PIECES):
        rows = pl.ds(k * FLAT, FLAT)
        v = dot(qs[2, :, k * FLAT : (k + 1) * FLAT], ps[2], 0, 0)
        ud[rows] = v.astype(BF16)
        nd[rows] = ((gd[rows].astype(F32) + ed[rows].astype(F32)) - v).astype(BF16)
        out(ud.at[rows], u2.at[rows])
        out(nd.at[rows], n2.at[rows])
    for cp in copies:
        cp.wait()


def finish(ps, qs, q, gm, em, gd, ed):
    inside = pl.BlockSpec(memory_space=pltpu.VMEM)
    outside = pl.BlockSpec(memory_space=pltpu.HBM)
    shapes = [(ROWS, D), (ROWS, D), (D, ROWS)]
    outs = [jax.ShapeDtypeStruct(shape, BF16) for shape in shapes]
    return pl.pallas_call(
        finish_kernel,
        name="finish",
        in_specs=[inside] * 7,
        out_specs=[outside] * 7,
        out_shape=outs + outs + [jax.ShapeDtypeStruct((3, RANK, D), F32)],
        scratch_shapes=[
            pltpu.VMEM((2, ROWS, D), BF16),
            pltpu.VMEM((2, ROWS, D), BF16),
            pltpu.VMEM((D, ROWS), BF16),
            pltpu.VMEM((D, ROWS), BF16),
            pltpu.SemaphoreType.DMA((6 * PIECES + 1,)),
        ],
        compiler_params=pltpu.CompilerParams(vmem_limit_bytes=24 << 20),
    )(ps, qs, q, gm, em, gd, ed)


def shards(gate_grad, up_grad, down_grad, gate_error, up_error, down_error, q_init):
    grads = (gate_grad[0], up_grad[0], down_grad[0])
    errors = (gate_error[0], up_error[0], down_error[0])
    pinned = [
        pltpu.with_memory_space_constraint(v, pltpu.HBM)
        for v in grads + errors + (jnp.swapaxes(q_init, 1, 2),)
    ]
    q, ps, qs, *held = exchange(*pinned)
    u0, u1, u2, n0, n1, n2, q_next = finish(ps, qs, q, *held)
    return u0, u1, u2, n0[None], n1[None], n2[None], jnp.swapaxes(q_next, 1, 2)


def solution(mesh):
    in_specs = (
        P("replica", "tensor", None),
        P("replica", "tensor", None),
        P("replica", None, "tensor"),
        P("replica", "tensor", None),
        P("replica", "tensor", None),
        P("replica", None, "tensor"),
        P(),
    )
    out_specs = (
        P("tensor", None),
        P("tensor", None),
        P(None, "tensor"),
        P("replica", "tensor", None),
        P("replica", "tensor", None),
        P("replica", None, "tensor"),
        P(),
    )
    return jax.shard_map(shards, mesh=mesh, in_specs=in_specs, out_specs=out_specs, check_vma=False)
```

```python
import jax
import jax.numpy as jnp
from jax import lax
from jax.experimental import pallas as pl
from jax.experimental.pallas import tpu as pltpu
from jax.sharding import PartitionSpec as P

ITERS = 2
D = 1024
RANK = 32
ROWS = 384
NY, NX, NZ = 4, 4, 8
MESH = pl.DeviceIdType.MESH
F32 = jnp.float32
BF16 = jnp.bfloat16
PARTS = 2

P_CORE, P_ONE, P_TWO, P_BACK, GRAM, Q_CORE, Q_SCATTER, Q_Z, Q_GATHER, Q_BACK = range(10)


def split(x, parts):
    out = []
    for k in range(parts):
        piece = x.astype(BF16)
        out.append(piece)
        if k + 1 < parts:
            x = x - piece.astype(F32)
    return out


def dot(a, b, ca, cb):
    return lax.dot_general(a, b, (((ca,), (cb,)), ((), ())), preferred_element_type=F32)


def small_left(a, cat_axis):
    h, m, l = split(a, 3)
    return jnp.concatenate([h, h, m, h, l, m], axis=cat_axis)


def small_right(b):
    h, m, l = split(b, 3)
    return jnp.concatenate([h, m, h, l, h, m], axis=0)


def fold(x, parts):
    total = x[(parts - 1) * RANK :]
    for k in range(parts - 2, -1, -1):
        total = total + x[k * RANK : (k + 1) * RANK]
    return total


def inverse_factors(grams):
    row = lax.broadcasted_iota(jnp.int32, (RANK, 2 * RANK), 0)
    lane = lax.broadcasted_iota(jnp.int32, (RANK, 2 * RANK), 1)
    eye = (lane == row + RANK).astype(F32)
    augs = []
    for g in grams:
        augs.append(jnp.concatenate([g, jnp.zeros_like(g)], axis=1) + eye)
    for j in range(RANK):
        for n in range(len(augs)):
            a = augs[n]
            pivot = a[j : j + 1, j : j + 1]
            r = lax.rsqrt(pivot)
            r = r * (1.5 - 0.5 * pivot * r * r)
            top = a[j : j + 1, :] * r
            col = a[:, j : j + 1] * r
            a = jnp.where(row > j, a - col * top, jnp.where(row == j, top, a))
            augs[n] = a
    return [a[:, RANK:] for a in augs]


def kernel(
    g0, g1, g2, e0, e1, e2, q0,
    q_out, ps_out, qs_out, gm, em, gd, ed,
    qi, qs, pt, pc, x1, x2, pf, gz, qp, qc, qsum, qr, zq, qf, linv,
    load, ssem, rsem, know,
):
    r = lax.axis_index("replica")
    z = lax.axis_index("tensor")
    y, x, c = r // 8, (r // 2) % 4, r % 2
    p = y * 4 + x
    other = 1 - c
    sib = (y * 8 + x * 2 + other, z)

    def at(yy, xx):
        return (yy * 8 + xx * 2 + c, z)

    plane = [
        ((y + dy) % NY, (x + dx) % NX)
        for dy, dx in [
            (2, 2), (2, 1), (1, 2), (2, 3), (3, 2), (1, 1), (1, 3), (3, 1), (3, 3),
            (2, 0), (0, 2), (1, 0), (0, 1), (3, 0), (0, 3),
        ]
    ]
    column = [(r, (z + dz) % NZ) for dz in (4, 3, 5, 2, 6, 1, 7)]
    xs = [at(y, (x + d) % NX) for d in (2, 1, 3)]
    ys = [at((y + d) % NY, x) for d in (2, 1, 3)]

    barrier = pltpu.get_barrier_semaphore()
    near = [(r, (z + dz) % NZ) for dz in (1, 7)]
    next_near = [(r, (z + dz) % NZ) for dz in (2, 6)]
    greet = xs + ys + near + [sib]
    for dev in greet:
        pl.semaphore_signal(barrier, inc=1, device_id=dev, device_id_type=MESH)

    loads = []
    for i, (src, dst) in enumerate(
        [(g0, gm.at[0]), (e0, em.at[0]), (g1, gm.at[1]), (e1, em.at[1]), (g2, gd), (e2, ed), (q0, qi)]
    ):
        cp = pltpu.make_async_copy(src, dst, load.at[i])
        loads.append(cp)
    for k in (6, 0, 1, 2, 3, 4, 5):
        loads[k].start()

    def send(stage, t, i, src, dst, dev):
        pltpu.make_async_remote_copy(
            src_ref=src,
            dst_ref=dst,
            send_sem=ssem.at[stage, t],
            recv_sem=rsem.at[stage, t, i],
            device_id=dev,
            device_id_type=MESH,
        ).start()

    def arrived(stage, t, i, like):
        pltpu.make_async_copy(like, like, rsem.at[stage, t, i]).wait()

    loads[6].wait()
    for i in range(3):
        qs[i] = jnp.concatenate(split(qi[i], PARTS), axis=0)

    def project(i):
        if i == 2:
            v = dot(qs[i], gd[...], 1, 0) + dot(qs[i], ed[...], 1, 0)
        else:
            v = dot(qs[i], gm[i], 1, 1) + dot(qs[i], em[i], 1, 1)
        return fold(v, PARTS) * (1.0 / 32.0)

    def back_project(i, ps):
        if i == 2:
            v = dot(ps, gd[...], 1, 1) + dot(ps, ed[...], 1, 1)
        else:
            v = dot(ps, gm[i], 1, 0) + dot(ps, em[i], 1, 0)
        return fold(v, PARTS) * (1.0 / 32.0)

    def tell(k, devs):
        for dev in devs:
            pl.semaphore_signal(know.at[k], inc=1, device_id=dev, device_id_type=MESH)

    def project_and_send(t, i):
        pt[t, i] = project(i).reshape(4, 8, ROWS)
        if t == 0 and i == 0:
            pl.semaphore_wait(barrier, len(greet))
        send(P_CORE, t, i, pt.at[t, i, pl.ds(2 * other, 2)], pc.at[t, i], sib)

    for i in range(3):
        loads[2 * i].wait()
        loads[2 * i + 1].wait()
        project_and_send(0, i)
    tell(0, near)

    def iteration(t, first):
        for i in range(3):
            arrived(P_CORE, t, i, pc.at[t, i])
            s = pt[t, i, pl.ds(2 * c, 2)] + pc[t, i]
            x1[t, i, 0, x] = s[0]
            x1[t, i, 1, y] = s[1]
            for dev in xs:
                send(P_ONE, t, i, x1.at[t, i, 0, x], x1.at[t, i, 0, x], dev)
            for dev in ys:
                send(P_ONE, t, i, x1.at[t, i, 1, y], x1.at[t, i, 1, y], dev)
        for i in range(3):
            arrived(P_ONE, t, i, x1.at[t, i, :, pl.ds(0, 3)])
            a = (x1[t, i, 0, 0] + x1[t, i, 0, 1]) + (x1[t, i, 0, 2] + x1[t, i, 0, 3])
            b = (x1[t, i, 1, 0] + x1[t, i, 1, 1]) + (x1[t, i, 1, 2] + x1[t, i, 1, 3])
            x2[t, i, 0, y] = a
            x2[t, i, 1, x] = b
            for dev in ys:
                send(P_TWO, t, i, x2.at[t, i, 0, y], x2.at[t, i, 0, y], dev)
            for dev in xs:
                send(P_TWO, t, i, x2.at[t, i, 1, x], x2.at[t, i, 1, x], dev)
        if first:
            pl.semaphore_wait(know.at[0], 2)
            tell(1, next_near)
        for i in range(3):
            arrived(P_TWO, t, i, x2.at[t, i, :, pl.ds(0, 3)])
            a = (x2[t, i, 0, 0] + x2[t, i, 0, 1]) + (x2[t, i, 0, 2] + x2[t, i, 0, 3])
            b = (x2[t, i, 1, 0] + x2[t, i, 1, 1]) + (x2[t, i, 1, 2] + x2[t, i, 1, 3])
            pf[t, i, 2 * c] = a
            pf[t, i, 2 * c + 1] = b
            send(P_BACK, t, i, pf.at[t, i, pl.ds(2 * c, 2)], pf.at[t, i, pl.ds(2 * c, 2)], sib)
        if first:
            pl.semaphore_wait(know.at[1], 2)
        grams = []
        for i in range(3):
            arrived(P_BACK, t, i, pf.at[t, i, pl.ds(0, 2)])
            ps = jnp.concatenate(split(pf[t, i].reshape(RANK, ROWS), PARTS), axis=0)
            term = back_project(i, ps)
            qp[t, i] = term.reshape(2, 2, 8, D)
            send(Q_CORE, t, i, qp.at[t, i, other], qc.at[t, i], sib)
            gg = fold(dot(ps, ps, 1, 1), PARTS)
            gram = gg[:, (PARTS - 1) * RANK :]
            for k in range(PARTS - 2, -1, -1):
                gram = gram + gg[:, k * RANK : (k + 1) * RANK]
            grams.append(gram)
        gz[t, z] = jnp.concatenate(grams + [jnp.zeros((RANK, RANK), F32)], axis=1)
        for dev in column:
            send(GRAM, t, 0, gz.at[t, z], gz.at[t, z], dev)
        for i in range(3):
            arrived(Q_CORE, t, i, qc.at[t, i])
            s = qp[t, i, c] + qc[t, i]
            for k in range(16):
                qsum[t, i, k] = s[k // 8, :, (k % 8) * 128 : (k % 8 + 1) * 128]
            qr[t, i, p] = qsum[t, i, p]
            for yy, xx in plane:
                send(Q_SCATTER, t, i, qsum.at[t, i, yy * 4 + xx], qr.at[t, i, p], at(yy, xx))
        for i in range(3):
            arrived(Q_SCATTER, t, i, qr.at[t, i, pl.ds(0, 15)])
            zq[t, i, z] = jnp.sum(qr[t, i], axis=0)
            for dev in column:
                send(Q_Z, t, i, zq.at[t, i, z], zq.at[t, i, z], dev)
        arrived(GRAM, t, 0, gz.at[t, pl.ds(0, 7)])
        gram = jnp.sum(gz[t], axis=0)
        inv = inverse_factors([gram[:, k * RANK : (k + 1) * RANK] for k in range(3)])
        for i in range(3):
            linv[i] = small_left(inv[i], 1)
        for i in range(3):
            arrived(Q_Z, t, i, zq.at[t, i, pl.ds(0, 7)])
            qf[t, i, c, p] = jnp.sum(zq[t, i], axis=0)
            for yy, xx in plane:
                send(Q_GATHER, t, i, qf.at[t, i, c, p], qf.at[t, i, c, p], at(yy, xx))
        if not first:
            for i in range(3):
                p_hat = dot(linv[i], small_right(pf[t, i].reshape(RANK, ROWS)), 1, 0)
                ph, pw = split(p_hat, 2)
                ps_out[i] = jnp.concatenate([ph, ph, pw], axis=0)
        for i in range(3):
            arrived(Q_GATHER, t, i, qf.at[t, i, 0, pl.ds(0, 15)])
            send(Q_BACK, t, i, qf.at[t, i, c], qf.at[t, i, c], sib)
        for i in range(3):
            arrived(Q_BACK, t, i, qf.at[t, i, 0])
            full = qf[t, i]
            raw = jnp.concatenate(
                [
                    jnp.concatenate([full[k // 2, (k % 2) * 8 + l] for l in range(8)], axis=1)
                    for k in range(4)
                ],
                axis=0,
            )
            q_now = dot(linv[i], small_right(raw), 1, 0)
            if first:
                qs[i] = jnp.concatenate(split(q_now, PARTS), axis=0)
                project_and_send(t + 1, i)
            else:
                q_out[i] = q_now
                qh, ql = split(q_now, 2)
                qs_out[i] = jnp.concatenate([qh, ql, qh], axis=0)

    for t in range(ITERS):
        iteration(t, t == 0)

    def sent(stage, t, like):
        pltpu.make_async_copy(like, like, ssem.at[stage, t]).wait()

    for t in range(ITERS):
        sent(P_CORE, t, pc.at[t])
        sent(P_ONE, t, x1.at[t, :, :, pl.ds(0, 3)])
        sent(P_TWO, t, x2.at[t, :, :, pl.ds(0, 3)])
        sent(P_BACK, t, pf.at[t, :, pl.ds(0, 2)])
        sent(GRAM, t, gz.at[t, pl.ds(0, 7)])
        sent(Q_CORE, t, qc.at[t])
        sent(Q_SCATTER, t, qr.at[t, :, pl.ds(0, 15)])
        sent(Q_Z, t, zq.at[t, :, pl.ds(0, 7)])
        sent(Q_GATHER, t, qf.at[t, :, 0, pl.ds(0, 15)])
        sent(Q_BACK, t, qf.at[t, :, 0])


def exchange(*operands):
    vmem = lambda *shape: pltpu.VMEM(shape, F32)
    scratch = [
        vmem(3, RANK, D),
        pltpu.VMEM((3, PARTS * RANK, D), BF16),
        vmem(ITERS, 3, 4, 8, ROWS),
        vmem(ITERS, 3, 2, 8, ROWS),
        vmem(ITERS, 3, 2, 4, 8, ROWS),
        vmem(ITERS, 3, 2, 4, 8, ROWS),
        vmem(ITERS, 3, 4, 8, ROWS),
        vmem(ITERS, NZ, RANK, 128),
        vmem(ITERS, 3, 2, 2, 8, D),
        vmem(ITERS, 3, 2, 8, D),
        vmem(ITERS, 3, 16, 8, 128),
        vmem(ITERS, 3, 16, 8, 128),
        vmem(ITERS, 3, NZ, 8, 128),
        vmem(ITERS, 3, 2, 16, 8, 128),
        pltpu.VMEM((3, RANK, 6 * RANK), BF16),
        pltpu.SemaphoreType.DMA((7,)),
        pltpu.SemaphoreType.DMA((10, ITERS)),
        pltpu.SemaphoreType.DMA((10, ITERS, 3)),
        pltpu.SemaphoreType.REGULAR((2,)),
    ]
    outside = pl.BlockSpec(memory_space=pltpu.HBM)
    inside = pl.BlockSpec(memory_space=pltpu.VMEM)
    return pl.pallas_call(
        kernel,
        name="power",
        out_shape=(
            jax.ShapeDtypeStruct((3, RANK, D), F32),
            jax.ShapeDtypeStruct((3, 3 * RANK, ROWS), BF16),
            jax.ShapeDtypeStruct((3, 3 * RANK, D), BF16),
            jax.ShapeDtypeStruct((2, ROWS, D), BF16),
            jax.ShapeDtypeStruct((2, ROWS, D), BF16),
            jax.ShapeDtypeStruct((D, ROWS), BF16),
            jax.ShapeDtypeStruct((D, ROWS), BF16),
        ),
        in_specs=[outside] * 7,
        out_specs=(inside,) * 7,
        scratch_shapes=scratch,
        compiler_params=pltpu.CompilerParams(
            collective_id=0, has_side_effects=True, vmem_limit_bytes=24 << 20
        ),
        cost_estimate=pl.CostEstimate(flops=10**9, bytes_accessed=6 * 10**6, transcendentals=0),
    )(*operands)


PIECES = 4
TALL = ROWS // PIECES
FLAT = D // PIECES


def finish_kernel(ps, qs, q, gm, em, gd, ed, u0, u1, u2, n0, n1, n2, q_out, um, nm, ud, nd, sem):
    copies = []

    def out(src, dst):
        cp = pltpu.make_async_copy(src, dst, sem.at[len(copies)])
        cp.start()
        copies.append(cp)

    out(q, q_out)
    for i, (u, n) in enumerate(((u0, n0), (u1, n1))):
        for k in range(PIECES):
            rows = pl.ds(k * TALL, TALL)
            v = dot(ps[i, :, k * TALL : (k + 1) * TALL], qs[i], 0, 0)
            um[i, rows] = v.astype(BF16)
            nm[i, rows] = ((gm[i, rows].astype(F32) + em[i, rows].astype(F32)) - v).astype(BF16)
            out(um.at[i, rows], u.at[rows])
            out(nm.at[i, rows], n.at[rows])
    for k in range(PIECES):
        rows = pl.ds(k * FLAT, FLAT)
        v = dot(qs[2, :, k * FLAT : (k + 1) * FLAT], ps[2], 0, 0)
        ud[rows] = v.astype(BF16)
        nd[rows] = ((gd[rows].astype(F32) + ed[rows].astype(F32)) - v).astype(BF16)
        out(ud.at[rows], u2.at[rows])
        out(nd.at[rows], n2.at[rows])
    for cp in copies:
        cp.wait()


def finish(ps, qs, q, gm, em, gd, ed):
    inside = pl.BlockSpec(memory_space=pltpu.VMEM)
    outside = pl.BlockSpec(memory_space=pltpu.HBM)
    shapes = [(ROWS, D), (ROWS, D), (D, ROWS)]
    outs = [jax.ShapeDtypeStruct(shape, BF16) for shape in shapes]
    return pl.pallas_call(
        finish_kernel,
        name="finish",
        in_specs=[inside] * 7,
        out_specs=[outside] * 7,
        out_shape=outs + outs + [jax.ShapeDtypeStruct((3, RANK, D), F32)],
        scratch_shapes=[
            pltpu.VMEM((2, ROWS, D), BF16),
            pltpu.VMEM((2, ROWS, D), BF16),
            pltpu.VMEM((D, ROWS), BF16),
            pltpu.VMEM((D, ROWS), BF16),
            pltpu.SemaphoreType.DMA((6 * PIECES + 1,)),
        ],
        compiler_params=pltpu.CompilerParams(vmem_limit_bytes=24 << 20),
    )(ps, qs, q, gm, em, gd, ed)


def shards(gate_grad, up_grad, down_grad, gate_error, up_error, down_error, q_init):
    grads = (gate_grad[0], up_grad[0], down_grad[0])
    errors = (gate_error[0], up_error[0], down_error[0])
    pinned = [
        pltpu.with_memory_space_constraint(v, pltpu.HBM)
        for v in grads + errors + (jnp.swapaxes(q_init, 1, 2),)
    ]
    q, ps, qs, *held = exchange(*pinned)
    u0, u1, u2, n0, n1, n2, q_next = finish(ps, qs, q, *held)
    return u0, u1, u2, n0[None], n1[None], n2[None], jnp.swapaxes(q_next, 1, 2)


def solution(mesh):
    in_specs = (
        P("replica", "tensor", None),
        P("replica", "tensor", None),
        P("replica", None, "tensor"),
        P("replica", "tensor", None),
        P("replica", "tensor", None),
        P("replica", None, "tensor"),
        P(),
    )
    out_specs = (
        P("tensor", None),
        P("tensor", None),
        P(None, "tensor"),
        P("replica", "tensor", None),
        P("replica", "tensor", None),
        P("replica", None, "tensor"),
        P(),
    )
    return jax.shard_map(shards, mesh=mesh, in_specs=in_specs, out_specs=out_specs, check_vma=False)
```

```python
import jax
import jax.numpy as jnp
from jax import lax
from jax.experimental import pallas as pl
from jax.experimental.pallas import tpu as pltpu
from jax.sharding import PartitionSpec as P

ITERS = 2
D = 1024
RANK = 32
ROWS = 384
NY, NX, NZ = 4, 4, 8
MESH = pl.DeviceIdType.MESH
F32 = jnp.float32
BF16 = jnp.bfloat16
PARTS = 2

(
    P_CORE, P_ONE, P_TWO, P_BACK, GRAM_1, Q_CORE, Q_SCATTER, Q_Z_1, Q_TILE,
    M_CORE, M_A, M_B, M_C,
    P_SUM, P_SHARE, GRAM_2, Q_SUM, Q_Z_2, Q_GATHER, Q_BACK,
) = range(20)
QUART = 96
HALF = 48


def split(x, parts):
    out = []
    for k in range(parts):
        piece = x.astype(BF16)
        out.append(piece)
        if k + 1 < parts:
            x = x - piece.astype(F32)
    return out


def dot(a, b, ca, cb):
    return lax.dot_general(a, b, (((ca,), (cb,)), ((), ())), preferred_element_type=F32)


def small_left(a, cat_axis):
    h, m, l = split(a, 3)
    return jnp.concatenate([h, h, m, h, l, m], axis=cat_axis)


def small_right(b):
    h, m, l = split(b, 3)
    return jnp.concatenate([h, m, h, l, h, m], axis=0)


def fold(x, parts):
    total = x[(parts - 1) * RANK :]
    for k in range(parts - 2, -1, -1):
        total = total + x[k * RANK : (k + 1) * RANK]
    return total


def inverse_factors(grams):
    row = lax.broadcasted_iota(jnp.int32, (RANK, 2 * RANK), 0)
    lane = lax.broadcasted_iota(jnp.int32, (RANK, 2 * RANK), 1)
    eye = (lane == row + RANK).astype(F32)
    augs = []
    for g in grams:
        augs.append(jnp.concatenate([g, jnp.zeros_like(g)], axis=1) + eye)
    for j in range(RANK):
        for n in range(len(augs)):
            a = augs[n]
            pivot = a[j : j + 1, j : j + 1]
            r = lax.rsqrt(pivot)
            r = r * (1.5 - 0.5 * pivot * r * r)
            top = a[j : j + 1, :] * r
            col = a[:, j : j + 1] * r
            a = jnp.where(row > j, a - col * top, jnp.where(row == j, top, a))
            augs[n] = a
    return [a[:, RANK:] for a in augs]


def kernel(
    g0, g1, g2, e0, e1, e2, q0,
    q_out, ps_out, qs_out, gm, em, gd, ed,
    qi, qs, pt, pc, x1, x2, pf, gz, qp, qc, qsum, qr, zq, qt, qtr, linv,
    wb, wr, ra, rb, rc, mean, px, pa, pw, qx, qxr, qf,
    load, ssem, rsem, know,
):
    r = lax.axis_index("replica")
    z = lax.axis_index("tensor")
    y, x, c = r // 8, (r // 2) % 4, r % 2
    p = y * 4 + x
    other = 1 - c
    sib = (y * 8 + x * 2 + other, z)

    def at(yy, xx):
        return (yy * 8 + xx * 2 + c, z)

    plane = [
        ((y + dy) % NY, (x + dx) % NX)
        for dy, dx in [
            (2, 2), (2, 1), (1, 2), (2, 3), (3, 2), (1, 1), (1, 3), (3, 1), (3, 3),
            (2, 0), (0, 2), (1, 0), (0, 1), (3, 0), (0, 3),
        ]
    ]
    column = [(r, (z + dz) % NZ) for dz in (4, 3, 5, 2, 6, 1, 7)]
    xs = [at(y, (x + d) % NX) for d in (2, 1, 3)]
    ys = [at((y + d) % NY, x) for d in (2, 1, 3)]
    yhi, ylo = y // 2, y % 2
    yy1 = yhi * 2 + (1 - ylo)
    rows_group = [at(yy1, (x + d) % NX) for d in (2, 1, 3, 0)] + xs
    yopp = (y + 2) % NY
    lanes_group = [
        (1 - yhi, other, (yopp * 8 + x * 2 + other, z)),
        (1 - yhi, c, at(yopp, x)),
        (yhi, other, sib),
    ]
    rank_group = 2 * c + yhi

    barrier = pltpu.get_barrier_semaphore()
    near = [(r, (z + dz) % NZ) for dz in (1, 7)]
    next_near = [(r, (z + dz) % NZ) for dz in (2, 6)]
    greet = xs + ys + near + [sib]
    for dev in greet:
        pl.semaphore_signal(barrier, inc=1, device_id=dev, device_id_type=MESH)

    loads = []
    for i, (src, dst) in enumerate(
        [(g0, gm.at[0]), (e0, em.at[0]), (g1, gm.at[1]), (e1, em.at[1]), (g2, gd), (e2, ed), (q0, qi)]
    ):
        cp = pltpu.make_async_copy(src, dst, load.at[i])
        loads.append(cp)
    for k in (6, 0, 1, 2, 3, 4, 5):
        loads[k].start()

    def send(stage, i, src, dst, dev):
        pltpu.make_async_remote_copy(
            src_ref=src,
            dst_ref=dst,
            send_sem=ssem.at[stage],
            recv_sem=rsem.at[stage, i],
            device_id=dev,
            device_id_type=MESH,
        ).start()

    def arrived(stage, i, like):
        pltpu.make_async_copy(like, like, rsem.at[stage, i]).wait()

    def sent(stage, like):
        pltpu.make_async_copy(like, like, ssem.at[stage]).wait()

    def tell(k, devs):
        for dev in devs:
            pl.semaphore_signal(know.at[k], inc=1, device_id=dev, device_id_type=MESH)

    place = ((x, y), (y, x))
    step = ((xs[1], xs[2]), (ys[1], ys[2]))
    own = wb.at[c]

    def mean_core(i):
        def put(rows_from, lanes_from, v):
            quarter, h = rows_from // QUART, (rows_from // HALF) % 2
            for k in range(v.shape[1] // 128):
                tile = lanes_from // 128 + k
                ty, tx = (quarter // 2) * 2 + tile // 4, tile % 4
                a, b = (tx, ty) if h == 0 else (ty, tx)
                wb[quarter % 2, i, h, a, b] = v[:, k * 128 : (k + 1) * 128]

        if i == 2:
            for tile in range(8):
                f = slice(tile * 128, (tile + 1) * 128)
                v = (gd[f].astype(F32) + ed[f].astype(F32)) * (1.0 / 32.0)
                v = v.T
                for k in range(8):
                    put(k * HALF, tile * 128, v[k * HALF : (k + 1) * HALF])
        else:
            for k in range(8):
                f = slice(k * HALF, (k + 1) * HALF)
                put(k * HALF, 0, (gm[i, f].astype(F32) + em[i, f].astype(F32)) * (1.0 / 32.0))
        send(M_CORE, i, wb.at[other, i], wr.at[i], sib)

    def mean_a(i):
        arrived(M_CORE, i, wr.at[i])
        wb[c, i] = wb[c, i] + wr[i]
        for h in range(2):
            a, _ = place[h]
            plus, minus = step[h]
            send(M_A, i, own.at[i, h, (a + 2) % 4, pl.ds(0, 2)], ra.at[i, h, 0], plus)
            send(M_A, i, own.at[i, h, (a + 2) % 4, pl.ds(2, 2)], ra.at[i, h, 1], minus)

    def mean_b(i):
        arrived(M_A, i, ra.at[i])
        for h in range(2):
            a, _ = place[h]
            up, down = (a + 1) % 4, (a + 3) % 4
            plus, minus = step[h]
            wb[c, i, h, up, pl.ds(0, 2)] = wb[c, i, h, up, pl.ds(0, 2)] + ra[i, h, 0]
            wb[c, i, h, down, pl.ds(2, 2)] = wb[c, i, h, down, pl.ds(2, 2)] + ra[i, h, 1]
            send(M_B, i, own.at[i, h, up], rb.at[i, h, 0], plus)
            send(M_B, i, own.at[i, h, down], rb.at[i, h, 1], minus)

    def mean_c(i):
        arrived(M_B, i, rb.at[i])
        for h in range(2):
            a, b = place[h]
            wb[c, i, h, a] = wb[c, i, h, a] + rb[i, h, 0] + rb[i, h, 1]
            for k in range(3):
                d = (2, 1, 3)[k]
                dev = (ys, xs)[h][k]
                send(M_C, i, own.at[i, h, a, (b + d) % 4], rc.at[i, h, k], dev)

    def mean_d(i):
        arrived(M_C, i, rc.at[i])
        for h in range(2):
            a, b = place[h]
            v = wb[c, i, h, a, b] + rc[i, h, 0] + (rc[i, h, 1] + rc[i, h, 2])
            hi, lo = split(v, 2)
            mean[i, 0, h * HALF : (h + 1) * HALF] = hi
            mean[i, 1, h * HALF : (h + 1) * HALF] = lo

    loads[6].wait()
    for i in range(3):
        qs[i] = jnp.concatenate(split(qi[i], PARTS), axis=0)

    def project(i):
        if i == 2:
            v = dot(qs[i], gd[...], 1, 0) + dot(qs[i], ed[...], 1, 0)
        else:
            v = dot(qs[i], gm[i], 1, 1) + dot(qs[i], em[i], 1, 1)
        return fold(v, PARTS) * (1.0 / 32.0)

    def back_project(i, ps):
        if i == 2:
            v = dot(ps, gd[...], 1, 1) + dot(ps, ed[...], 1, 1)
        else:
            v = dot(ps, gm[i], 1, 0) + dot(ps, em[i], 1, 0)
        return fold(v, PARTS) * (1.0 / 32.0)

    def gram_of(ps):
        gg = fold(dot(ps, ps, 1, 1), PARTS)
        gram = gg[:, (PARTS - 1) * RANK :]
        for k in range(PARTS - 2, -1, -1):
            gram = gram + gg[:, k * RANK : (k + 1) * RANK]
        return gram

    def gram_send(stage, t, grams):
        gz[t, z] = jnp.concatenate(grams + [jnp.zeros((RANK, RANK), F32)], axis=1)
        for dev in column:
            send(stage, 0, gz.at[t, z], gz.at[t, z], dev)

    def factors(stage, t):
        arrived(stage, 0, gz.at[t, pl.ds(0, 7)])
        gram = jnp.sum(gz[t], axis=0)
        inv = inverse_factors([gram[:, k * RANK : (k + 1) * RANK] for k in range(3)])
        for i in range(3):
            linv[i] = small_left(inv[i], 1)

    for i in range(3):
        loads[2 * i].wait()
        loads[2 * i + 1].wait()
        pt[i] = project(i).reshape(4, 8, ROWS)
        if i == 0:
            pl.semaphore_wait(barrier, len(greet))
        send(P_CORE, i, pt.at[i, pl.ds(2 * other, 2)], pc.at[i], sib)
    tell(0, near)
    mean_core(0)
    mean_core(1)
    for i in range(3):
        arrived(P_CORE, i, pc.at[i])
        s = pt[i, pl.ds(2 * c, 2)] + pc[i]
        x1[i, 0, x] = s[0]
        x1[i, 1, y] = s[1]
        for dev in xs:
            send(P_ONE, i, x1.at[i, 0, x], x1.at[i, 0, x], dev)
        for dev in ys:
            send(P_ONE, i, x1.at[i, 1, y], x1.at[i, 1, y], dev)
    mean_core(2)
    mean_a(0)
    for i in range(3):
        arrived(P_ONE, i, x1.at[i, :, pl.ds(0, 3)])
        a = (x1[i, 0, 0] + x1[i, 0, 1]) + (x1[i, 0, 2] + x1[i, 0, 3])
        b = (x1[i, 1, 0] + x1[i, 1, 1]) + (x1[i, 1, 2] + x1[i, 1, 3])
        x2[i, 0, y] = a
        x2[i, 1, x] = b
        for dev in ys:
            send(P_TWO, i, x2.at[i, 0, y], x2.at[i, 0, y], dev)
        for dev in xs:
            send(P_TWO, i, x2.at[i, 1, x], x2.at[i, 1, x], dev)
    pl.semaphore_wait(know.at[0], 2)
    tell(1, next_near)
    mean_a(1)
    mean_a(2)
    mean_b(0)
    for i in range(3):
        arrived(P_TWO, i, x2.at[i, :, pl.ds(0, 3)])
        a = (x2[i, 0, 0] + x2[i, 0, 1]) + (x2[i, 0, 2] + x2[i, 0, 3])
        b = (x2[i, 1, 0] + x2[i, 1, 1]) + (x2[i, 1, 2] + x2[i, 1, 3])
        pf[i, 2 * c] = a
        pf[i, 2 * c + 1] = b
        send(P_BACK, i, pf.at[i, pl.ds(2 * c, 2)], pf.at[i, pl.ds(2 * c, 2)], sib)
    pl.semaphore_wait(know.at[1], 2)
    grams = []
    for i in range(3):
        arrived(P_BACK, i, pf.at[i, pl.ds(0, 2)])
        ps = jnp.concatenate(split(pf[i].reshape(RANK, ROWS), PARTS), axis=0)
        qp[i] = back_project(i, ps).reshape(2, 2, 8, D)
        send(Q_CORE, i, qp.at[i, other], qc.at[i], sib)
        grams.append(gram_of(ps))
    gram_send(GRAM_1, 0, grams)
    for i in range(3):
        arrived(Q_CORE, i, qc.at[i])
        s = qp[i, c] + qc[i]
        for k in range(16):
            qsum[i, k] = s[k // 8, :, (k % 8) * 128 : (k % 8 + 1) * 128]
        qr[i, p] = qsum[i, p]
        for yy, xx in plane:
            send(Q_SCATTER, i, qsum.at[i, yy * 4 + xx], qr.at[i, p], at(yy, xx))
    mean_b(1)
    mean_b(2)
    for i in range(3):
        arrived(Q_SCATTER, i, qr.at[i, pl.ds(0, 15)])
        zq[0, i, z] = jnp.sum(qr[i], axis=0)
        for dev in column:
            send(Q_Z_1, i, zq.at[0, i, z], zq.at[0, i, z], dev)
    factors(GRAM_1, 0)
    for i in range(3):
        mean_c(i)
    for i in range(3):
        arrived(Q_Z_1, i, zq.at[0, i, pl.ds(0, 7)])
        qt[i, rank_group] = jnp.sum(zq[0, i], axis=0)
        for _, _, dev in lanes_group:
            send(Q_TILE, i, qt.at[i, rank_group], qt.at[i, rank_group], dev)
    for i in range(3):
        arrived(Q_TILE, i, qt.at[i, pl.ds(0, 3)])
        q_now = dot(linv[i], small_right(qt[i].reshape(RANK, 128)), 1, 0)
        qtr[i] = jnp.concatenate(split(q_now, PARTS), axis=0)
    for i in range(3):
        mean_d(i)
        v = fold(dot(qtr[i], mean[i, 0], 1, 1) + dot(qtr[i], mean[i, 1], 1, 1), PARTS)
        slot = ylo * 4 + x
        px[i, slot] = jnp.concatenate([v, jnp.zeros((RANK, 128 - QUART), F32)], axis=1)
        for dev in rows_group:
            send(P_SUM, i, px.at[i, slot], px.at[i, slot], dev)
    for i in range(3):
        arrived(P_SUM, i, px.at[i, pl.ds(0, 7)])
        v = jnp.sum(px[i], axis=0)
        quarter = yhi * 2 + c
        pa[i, quarter] = v
        for _, _, dev in lanes_group:
            send(P_SHARE, i, pa.at[i, quarter], pa.at[i, quarter], dev)
        ps = jnp.concatenate(split(v[:, :QUART], PARTS), axis=0)
        v = fold(dot(ps, mean[i, 0], 1, 0) + dot(ps, mean[i, 1], 1, 0), PARTS)
        qx[i] = v.reshape(4, 8, 128)
        qxr[i, rank_group] = qx[i, rank_group]
        for yh, cc, dev in lanes_group:
            send(Q_SUM, i, qx.at[i, 2 * cc + yh], qxr.at[i, rank_group], dev)
    grams = []
    for i in range(3):
        arrived(P_SHARE, i, pa.at[i, pl.ds(0, 3)])
        whole = jnp.concatenate([pa[i, k][:, :QUART] for k in range(4)], axis=1)
        pw[i] = whole
        grams.append(gram_of(jnp.concatenate(split(whole, PARTS), axis=0)))
    for i in range(3):
        arrived(Q_SUM, i, qxr.at[i, pl.ds(0, 3)])
        zq[1, i, z] = jnp.sum(qxr[i], axis=0)
        for dev in column:
            send(Q_Z_2, i, zq.at[1, i, z], zq.at[1, i, z], dev)
    gram_send(GRAM_2, 1, grams)
    for i in range(3):
        arrived(Q_Z_2, i, zq.at[1, i, pl.ds(0, 7)])
        qf[i, c, p] = jnp.sum(zq[1, i], axis=0)
        for yy, xx in plane:
            send(Q_GATHER, i, qf.at[i, c, p], qf.at[i, c, p], at(yy, xx))
    factors(GRAM_2, 1)
    for i in range(3):
        p_hat = dot(linv[i], small_right(pw[i]), 1, 0)
        ph, p_low = split(p_hat, 2)
        ps_out[i] = jnp.concatenate([ph, ph, p_low], axis=0)
    for i in range(3):
        arrived(Q_GATHER, i, qf.at[i, 0, pl.ds(0, 15)])
        send(Q_BACK, i, qf.at[i, c], qf.at[i, c], sib)
    for i in range(3):
        arrived(Q_BACK, i, qf.at[i, 0])
        full = qf[i]
        raw = jnp.concatenate(
            [
                jnp.concatenate([full[k // 2, (k % 2) * 8 + l] for l in range(8)], axis=1)
                for k in range(4)
            ],
            axis=0,
        )
        q_now = dot(linv[i], small_right(raw), 1, 0)
        q_out[i] = q_now
        qh, ql = split(q_now, 2)
        qs_out[i] = jnp.concatenate([qh, ql, qh], axis=0)

    sent(P_CORE, pc)
    sent(P_ONE, x1.at[:, :, pl.ds(0, 3)])
    sent(P_TWO, x2.at[:, :, pl.ds(0, 3)])
    sent(P_BACK, pf.at[:, pl.ds(0, 2)])
    sent(GRAM_1, gz.at[0, pl.ds(0, 7)])
    sent(Q_CORE, qc)
    sent(Q_SCATTER, qr.at[:, pl.ds(0, 15)])
    sent(Q_Z_1, zq.at[0, :, pl.ds(0, 7)])
    sent(Q_TILE, qt.at[:, pl.ds(0, 3)])
    sent(M_CORE, wr)
    sent(M_A, ra)
    sent(M_B, rb)
    sent(M_C, rc)
    sent(P_SUM, px.at[:, pl.ds(0, 7)])
    sent(P_SHARE, pa.at[:, pl.ds(0, 3)])
    sent(GRAM_2, gz.at[1, pl.ds(0, 7)])
    sent(Q_SUM, qxr.at[:, pl.ds(0, 3)])
    sent(Q_Z_2, zq.at[1, :, pl.ds(0, 7)])
    sent(Q_GATHER, qf.at[:, 0, pl.ds(0, 15)])
    sent(Q_BACK, qf.at[:, 0])


def exchange(*operands):
    vmem = lambda *shape: pltpu.VMEM(shape, F32)
    scratch = [
        vmem(3, RANK, D),
        pltpu.VMEM((3, PARTS * RANK, D), BF16),
        vmem(3, 4, 8, ROWS),
        vmem(3, 2, 8, ROWS),
        vmem(3, 2, 4, 8, ROWS),
        vmem(3, 2, 4, 8, ROWS),
        vmem(3, 4, 8, ROWS),
        vmem(ITERS, NZ, RANK, 128),
        vmem(3, 2, 2, 8, D),
        vmem(3, 2, 8, D),
        vmem(3, 16, 8, 128),
        vmem(3, 16, 8, 128),
        vmem(ITERS, 3, NZ, 8, 128),
        vmem(3, 4, 8, 128),
        pltpu.VMEM((3, PARTS * RANK, 128), BF16),
        pltpu.VMEM((3, RANK, 6 * RANK), BF16),
        vmem(2, 3, 2, 4, 4, HALF, 128),
        vmem(3, 2, 4, 4, HALF, 128),
        vmem(3, 2, 2, 2, HALF, 128),
        vmem(3, 2, 2, 4, HALF, 128),
        vmem(3, 2, 3, HALF, 128),
        pltpu.VMEM((3, 2, QUART, 128), BF16),
        vmem(3, 8, RANK, 128),
        vmem(3, 4, RANK, 128),
        vmem(3, RANK, ROWS),
        vmem(3, 4, 8, 128),
        vmem(3, 4, 8, 128),
        vmem(3, 2, 16, 8, 128),
        pltpu.SemaphoreType.DMA((7,)),
        pltpu.SemaphoreType.DMA((20,)),
        pltpu.SemaphoreType.DMA((20, 3)),
        pltpu.SemaphoreType.REGULAR((2,)),
    ]
    inside = pl.BlockSpec(memory_space=pltpu.VMEM)
    outside = pl.BlockSpec(memory_space=pltpu.HBM)
    return pl.pallas_call(
        kernel,
        name="power",
        out_shape=(
            jax.ShapeDtypeStruct((3, RANK, D), F32),
            jax.ShapeDtypeStruct((3, 3 * RANK, ROWS), BF16),
            jax.ShapeDtypeStruct((3, 3 * RANK, D), BF16),
            jax.ShapeDtypeStruct((2, ROWS, D), BF16),
            jax.ShapeDtypeStruct((2, ROWS, D), BF16),
            jax.ShapeDtypeStruct((D, ROWS), BF16),
            jax.ShapeDtypeStruct((D, ROWS), BF16),
        ),
        in_specs=[outside] * 7,
        out_specs=(inside,) * 7,
        scratch_shapes=scratch,
        compiler_params=pltpu.CompilerParams(
            collective_id=0, has_side_effects=True, vmem_limit_bytes=32 << 20
        ),
        cost_estimate=pl.CostEstimate(flops=10**9, bytes_accessed=6 * 10**6, transcendentals=0),
    )(*operands)


PIECES = 4
TALL = ROWS // PIECES
FLAT = D // PIECES


def finish_kernel(ps, qs, q, gm, em, gd, ed, u0, u1, u2, n0, n1, n2, q_out, um, nm, ud, nd, sem):
    copies = []

    def out(src, dst):
        cp = pltpu.make_async_copy(src, dst, sem.at[len(copies)])
        cp.start()
        copies.append(cp)

    out(q, q_out)
    for i, (u, n) in enumerate(((u0, n0), (u1, n1))):
        for k in range(PIECES):
            rows = pl.ds(k * TALL, TALL)
            v = dot(ps[i, :, k * TALL : (k + 1) * TALL], qs[i], 0, 0)
            um[i, rows] = v.astype(BF16)
            nm[i, rows] = ((gm[i, rows].astype(F32) + em[i, rows].astype(F32)) - v).astype(BF16)
            out(um.at[i, rows], u.at[rows])
            out(nm.at[i, rows], n.at[rows])
    for k in range(PIECES):
        rows = pl.ds(k * FLAT, FLAT)
        v = dot(qs[2, :, k * FLAT : (k + 1) * FLAT], ps[2], 0, 0)
        ud[rows] = v.astype(BF16)
        nd[rows] = ((gd[rows].astype(F32) + ed[rows].astype(F32)) - v).astype(BF16)
        out(ud.at[rows], u2.at[rows])
        out(nd.at[rows], n2.at[rows])
    for cp in copies:
        cp.wait()


def finish(ps, qs, q, gm, em, gd, ed):
    inside = pl.BlockSpec(memory_space=pltpu.VMEM)
    outside = pl.BlockSpec(memory_space=pltpu.HBM)
    shapes = [(ROWS, D), (ROWS, D), (D, ROWS)]
    outs = [jax.ShapeDtypeStruct(shape, BF16) for shape in shapes]
    return pl.pallas_call(
        finish_kernel,
        name="finish",
        in_specs=[inside] * 7,
        out_specs=[outside] * 7,
        out_shape=outs + outs + [jax.ShapeDtypeStruct((3, RANK, D), F32)],
        scratch_shapes=[
            pltpu.VMEM((2, ROWS, D), BF16),
            pltpu.VMEM((2, ROWS, D), BF16),
            pltpu.VMEM((D, ROWS), BF16),
            pltpu.VMEM((D, ROWS), BF16),
            pltpu.SemaphoreType.DMA((6 * PIECES + 1,)),
        ],
        compiler_params=pltpu.CompilerParams(vmem_limit_bytes=24 << 20),
    )(ps, qs, q, gm, em, gd, ed)


def shards(gate_grad, up_grad, down_grad, gate_error, up_error, down_error, q_init):
    grads = (gate_grad[0], up_grad[0], down_grad[0])
    errors = (gate_error[0], up_error[0], down_error[0])
    pinned = [
        pltpu.with_memory_space_constraint(v, pltpu.HBM)
        for v in grads + errors + (jnp.swapaxes(q_init, 1, 2),)
    ]
    q, ps, qs, *held = exchange(*pinned)
    u0, u1, u2, n0, n1, n2, q_next = finish(ps, qs, q, *held)
    return u0, u1, u2, n0[None], n1[None], n2[None], jnp.swapaxes(q_next, 1, 2)


def solution(mesh):
    in_specs = (
        P("replica", "tensor", None),
        P("replica", "tensor", None),
        P("replica", None, "tensor"),
        P("replica", "tensor", None),
        P("replica", "tensor", None),
        P("replica", None, "tensor"),
        P(),
    )
    out_specs = (
        P("tensor", None),
        P("tensor", None),
        P(None, "tensor"),
        P("replica", "tensor", None),
        P("replica", "tensor", None),
        P("replica", None, "tensor"),
        P(),
    )
    return jax.shard_map(shards, mesh=mesh, in_specs=in_specs, out_specs=out_specs, check_vma=False)
```

```python
import jax
import jax.numpy as jnp
from jax import lax
from jax.experimental import pallas as pl
from jax.experimental.pallas import tpu as pltpu
from jax.sharding import PartitionSpec as P

ITERS = 2
D = 1024
RANK = 32
ROWS = 384
NY, NX, NZ = 4, 4, 8
MESH = pl.DeviceIdType.MESH
F32 = jnp.float32
BF16 = jnp.bfloat16
PARTS = 2

(
    P_CORE, P_ONE, P_TWO, P_BACK, GRAM_1, Q_CORE, Q_SCATTER, Q_Z_1, Q_TILE,
    M_CORE, M_A, M_B, M_C,
    P_SUM, P_SHARE, GRAM_2, Q_SUM, Q_Z_2, Q_GATHER, Q_BACK,
) = range(20)
QUART = 96
HALF = 48


def split(x, parts):
    out = []
    for k in range(parts):
        piece = x.astype(BF16)
        out.append(piece)
        if k + 1 < parts:
            x = x - piece.astype(F32)
    return out


def dot(a, b, ca, cb):
    return lax.dot_general(a, b, (((ca,), (cb,)), ((), ())), preferred_element_type=F32)


def small_left(a, cat_axis):
    h, m, l = split(a, 3)
    return jnp.concatenate([h, h, m, h, l, m], axis=cat_axis)


def small_right(b):
    h, m, l = split(b, 3)
    return jnp.concatenate([h, m, h, l, h, m], axis=0)


def pack(v):
    tail = jnp.concatenate([v[24:, k * 32 : (k + 1) * 32] for k in range(3)], axis=0)
    return jnp.concatenate([v[:24], tail], axis=1)


def unpack(v):
    tail = jnp.concatenate([v[8 * k : 8 * k + 8, QUART:] for k in range(3)], axis=1)
    return jnp.concatenate([v[:, :QUART], tail], axis=0)


def fold(x, parts):
    total = x[(parts - 1) * RANK :]
    for k in range(parts - 2, -1, -1):
        total = total + x[k * RANK : (k + 1) * RANK]
    return total


def inverse_factors(grams):
    row = lax.broadcasted_iota(jnp.int32, (RANK, 2 * RANK), 0)
    lane = lax.broadcasted_iota(jnp.int32, (RANK, 2 * RANK), 1)
    eye = (lane == row + RANK).astype(F32)
    augs = []
    for g in grams:
        augs.append(jnp.concatenate([g, jnp.zeros_like(g)], axis=1) + eye)
    for j in range(RANK):
        for n in range(len(augs)):
            a = augs[n]
            pivot = a[j : j + 1, j : j + 1]
            r = lax.rsqrt(pivot)
            r = r * (1.5 - 0.5 * pivot * r * r)
            top = a[j : j + 1, :] * r
            col = a[:, j : j + 1] * r
            a = jnp.where(row > j, a - col * top, jnp.where(row == j, top, a))
            augs[n] = a
    return [a[:, RANK:] for a in augs]


def kernel(
    g0, g1, g2, e0, e1, e2, q0,
    q_out, ps_out, qs_out, gm, em, gd, ed,
    qi, qs, pt, pc, x1, x2, pf, gz, qp, qc, qsum, qr, zq, qt, qtr, linv,
    wb, wr, ra, rb, rc, mean, px, pa, pw, qx, qxr, qf,
    load, ssem, rsem, know,
):
    r = lax.axis_index("replica")
    z = lax.axis_index("tensor")
    y, x, c = r // 8, (r // 2) % 4, r % 2
    ps_index = (y * 4 + x, x * 4 + y, y * 4 + x)
    other = 1 - c
    sib = (y * 8 + x * 2 + other, z)

    def at(yy, xx):
        return (yy * 8 + xx * 2 + c, z)

    plane = [
        ((y + dy) % NY, (x + dx) % NX)
        for dy, dx in [
            (2, 2), (2, 1), (1, 2), (2, 3), (3, 2), (1, 1), (1, 3), (3, 1), (3, 3),
            (2, 0), (0, 2), (1, 0), (0, 1), (3, 0), (0, 3),
        ]
    ]
    column = [(r, (z + dz) % NZ) for dz in (4, 3, 5, 2, 6, 1, 7)]
    xs = [at(y, (x + d) % NX) for d in (2, 1, 3)]
    ys = [at((y + d) % NY, x) for d in (2, 1, 3)]
    yflip, xflip = (y // 2) * 2 + (1 - y % 2), (x // 2) * 2 + (1 - x % 2)
    along_x = [at(yflip, (x + d) % NX) for d in (2, 1, 3, 0)] + xs
    along_y = [at((y + d) % NY, xflip) for d in (2, 1, 3, 0)] + ys
    rows_group = (along_x, along_y, along_x)
    yopp, xopp = (y + 2) % NY, (x + 2) % NX

    def four(high, yy, xx):
        return [
            (1 - high, other, (yy * 8 + xx * 2 + other, z)),
            (1 - high, c, at(yy, xx)),
            (high, other, sib),
        ]

    lanes_group = (four(y // 2, yopp, x), four(x // 2, y, xopp), four(y // 2, yopp, x))
    highs, slots = (y // 2, x // 2, y // 2), ((y % 2) * 4 + x, (x % 2) * 4 + y, (y % 2) * 4 + x)
    rank_groups = [2 * c + high for high in highs]

    barrier = pltpu.get_barrier_semaphore()
    near = [(r, (z + dz) % NZ) for dz in (1, 7)]
    next_near = [(r, (z + dz) % NZ) for dz in (2, 6)]
    greet = xs + ys + near + [sib]
    for dev in greet:
        pl.semaphore_signal(barrier, inc=1, device_id=dev, device_id_type=MESH)

    loads = []
    for i, (src, dst) in enumerate(
        [(g0, gm.at[0]), (e0, em.at[0]), (g1, gm.at[1]), (e1, em.at[1]), (g2, gd), (e2, ed), (q0, qi)]
    ):
        cp = pltpu.make_async_copy(src, dst, load.at[i])
        loads.append(cp)
    for k in (6, 0, 1, 2, 3, 4, 5):
        loads[k].start()

    def send(stage, i, src, dst, dev):
        pltpu.make_async_remote_copy(
            src_ref=src,
            dst_ref=dst,
            send_sem=ssem.at[stage],
            recv_sem=rsem.at[stage, i],
            device_id=dev,
            device_id_type=MESH,
        ).start()

    def arrived(stage, i, like):
        pltpu.make_async_copy(like, like, rsem.at[stage, i]).wait()

    def sent(stage, like):
        pltpu.make_async_copy(like, like, ssem.at[stage]).wait()

    def tell(k, devs):
        for dev in devs:
            pl.semaphore_signal(know.at[k], inc=1, device_id=dev, device_id_type=MESH)

    place = ((x, y), (y, x))
    step = ((xs[1], xs[2]), (ys[1], ys[2]))
    own = wb.at[c]

    def mean_core(i):
        def put(rows_from, lanes_from, v):
            quarter, h = rows_from // QUART, (rows_from // HALF) % 2
            for k in range(v.shape[1] // 128):
                tile = lanes_from // 128 + k
                ty, tx = (quarter // 2) * 2 + tile // 4, tile % 4
                a, b = (tx, ty) if (h == 0) == (i != 1) else (ty, tx)
                wb[quarter % 2, i, h, a, b] = v[:, k * 128 : (k + 1) * 128]

        if i == 2:
            for tile in range(8):
                f = slice(tile * 128, (tile + 1) * 128)
                v = (gd[f].astype(F32) + ed[f].astype(F32)) * (1.0 / 32.0)
                v = v.T
                for k in range(8):
                    put(k * HALF, tile * 128, v[k * HALF : (k + 1) * HALF])
        else:
            for k in range(8):
                f = slice(k * HALF, (k + 1) * HALF)
                put(k * HALF, 0, (gm[i, f].astype(F32) + em[i, f].astype(F32)) * (1.0 / 32.0))
        send(M_CORE, i, wb.at[other, i], wr.at[i], sib)

    def mean_a(i):
        arrived(M_CORE, i, wr.at[i])
        wb[c, i] = wb[c, i] + wr[i]
        for h in range(2):
            a, _ = place[h]
            plus, minus = step[h]
            send(M_A, i, own.at[i, h, (a + 2) % 4, pl.ds(0, 2)], ra.at[i, h, 0], plus)
            send(M_A, i, own.at[i, h, (a + 2) % 4, pl.ds(2, 2)], ra.at[i, h, 1], minus)

    def mean_b(i):
        arrived(M_A, i, ra.at[i])
        for h in range(2):
            a, _ = place[h]
            up, down = (a + 1) % 4, (a + 3) % 4
            plus, minus = step[h]
            wb[c, i, h, up, pl.ds(0, 2)] = wb[c, i, h, up, pl.ds(0, 2)] + ra[i, h, 0]
            wb[c, i, h, down, pl.ds(2, 2)] = wb[c, i, h, down, pl.ds(2, 2)] + ra[i, h, 1]
            send(M_B, i, own.at[i, h, up], rb.at[i, h, 0], plus)
            send(M_B, i, own.at[i, h, down], rb.at[i, h, 1], minus)

    def mean_c(i):
        arrived(M_B, i, rb.at[i])
        for h in range(2):
            a, b = place[h]
            wb[c, i, h, a] = wb[c, i, h, a] + rb[i, h, 0] + rb[i, h, 1]
            for k in range(3):
                d = (2, 1, 3)[k]
                dev = (ys, xs)[h][k]
                send(M_C, i, own.at[i, h, a, (b + d) % 4], rc.at[i, h, k], dev)

    def mean_d(i):
        arrived(M_C, i, rc.at[i])
        for h in range(2):
            a, b = place[h]
            v = wb[c, i, h, a, b] + rc[i, h, 0] + (rc[i, h, 1] + rc[i, h, 2])
            hi, lo = split(v, 2)
            mean[i, 0, h * HALF : (h + 1) * HALF] = hi
            mean[i, 1, h * HALF : (h + 1) * HALF] = lo

    loads[6].wait()
    for i in range(3):
        qs[i] = jnp.concatenate(split(qi[i], PARTS), axis=0)

    def project(i):
        if i == 2:
            v = dot(qs[i], gd[...], 1, 0) + dot(qs[i], ed[...], 1, 0)
        else:
            v = dot(qs[i], gm[i], 1, 1) + dot(qs[i], em[i], 1, 1)
        return fold(v, PARTS) * (1.0 / 32.0)

    def back_project(i, ps):
        if i == 2:
            v = dot(ps, gd[...], 1, 1) + dot(ps, ed[...], 1, 1)
        else:
            v = dot(ps, gm[i], 1, 0) + dot(ps, em[i], 1, 0)
        return fold(v, PARTS) * (1.0 / 32.0)

    def gram_of(ps):
        gg = fold(dot(ps, ps, 1, 1), PARTS)
        gram = gg[:, (PARTS - 1) * RANK :]
        for k in range(PARTS - 2, -1, -1):
            gram = gram + gg[:, k * RANK : (k + 1) * RANK]
        return gram

    def gram_send(stage, t, grams):
        gz[t, z] = jnp.concatenate(grams + [jnp.zeros((RANK, RANK), F32)], axis=1)
        for dev in column:
            send(stage, 0, gz.at[t, z], gz.at[t, z], dev)

    def factors(stage, t):
        arrived(stage, 0, gz.at[t, pl.ds(0, 7)])
        gram = jnp.sum(gz[t], axis=0)
        inv = inverse_factors([gram[:, k * RANK : (k + 1) * RANK] for k in range(3)])
        for i in range(3):
            linv[i] = small_left(inv[i], 1)

    for i in range(3):
        loads[2 * i].wait()
        loads[2 * i + 1].wait()
        pt[i] = project(i).reshape(4, 8, ROWS)
        if i == 0:
            pl.semaphore_wait(barrier, len(greet))
        send(P_CORE, i, pt.at[i, pl.ds(2 * other, 2)], pc.at[i], sib)
    tell(0, near)
    mean_core(0)
    for i in range(3):
        arrived(P_CORE, i, pc.at[i])
        s = pt[i, pl.ds(2 * c, 2)] + pc[i]
        x1[i, 0, x] = s[0]
        x1[i, 1, y] = s[1]
        for dev in xs:
            send(P_ONE, i, x1.at[i, 0, x], x1.at[i, 0, x], dev)
        for dev in ys:
            send(P_ONE, i, x1.at[i, 1, y], x1.at[i, 1, y], dev)
    mean_core(1)
    mean_core(2)
    mean_a(0)
    for i in range(3):
        arrived(P_ONE, i, x1.at[i, :, pl.ds(0, 3)])
        a = (x1[i, 0, 0] + x1[i, 0, 1]) + (x1[i, 0, 2] + x1[i, 0, 3])
        b = (x1[i, 1, 0] + x1[i, 1, 1]) + (x1[i, 1, 2] + x1[i, 1, 3])
        x2[i, 0, y] = a
        x2[i, 1, x] = b
        for dev in ys:
            send(P_TWO, i, x2.at[i, 0, y], x2.at[i, 0, y], dev)
        for dev in xs:
            send(P_TWO, i, x2.at[i, 1, x], x2.at[i, 1, x], dev)
    pl.semaphore_wait(know.at[0], 2)
    tell(1, next_near)
    mean_a(1)
    mean_a(2)
    mean_b(0)
    for i in range(3):
        arrived(P_TWO, i, x2.at[i, :, pl.ds(0, 3)])
        a = (x2[i, 0, 0] + x2[i, 0, 1]) + (x2[i, 0, 2] + x2[i, 0, 3])
        b = (x2[i, 1, 0] + x2[i, 1, 1]) + (x2[i, 1, 2] + x2[i, 1, 3])
        pf[i, 2 * c] = a
        pf[i, 2 * c + 1] = b
        send(P_BACK, i, pf.at[i, pl.ds(2 * c, 2)], pf.at[i, pl.ds(2 * c, 2)], sib)
    pl.semaphore_wait(know.at[1], 2)
    grams = []
    for i in range(3):
        arrived(P_BACK, i, pf.at[i, pl.ds(0, 2)])
        ps = jnp.concatenate(split(pf[i].reshape(RANK, ROWS), PARTS), axis=0)
        qp[i] = back_project(i, ps).reshape(2, 2, 8, D)
        send(Q_CORE, i, qp.at[i, other], qc.at[i], sib)
        grams.append(gram_of(ps))
    gram_send(GRAM_1, 0, grams)
    for i in range(3):
        arrived(Q_CORE, i, qc.at[i])
        s = qp[i, c] + qc[i]
        for k in range(16):
            qsum[i, k] = s[k // 8, :, (k % 8) * 128 : (k % 8 + 1) * 128]
        p = ps_index[i]
        qr[i, p] = qsum[i, p]
        for yy, xx in plane:
            there = xx * 4 + yy if i == 1 else yy * 4 + xx
            send(Q_SCATTER, i, qsum.at[i, there], qr.at[i, p], at(yy, xx))
    mean_b(1)
    mean_b(2)
    for i in range(3):
        arrived(Q_SCATTER, i, qr.at[i, pl.ds(0, 15)])
        zq[0, i, z] = jnp.sum(qr[i], axis=0)
        for dev in column:
            send(Q_Z_1, i, zq.at[0, i, z], zq.at[0, i, z], dev)
    mean_c(0)
    factors(GRAM_1, 0)
    for i in range(1, 3):
        mean_c(i)
    for i in range(3):
        arrived(Q_Z_1, i, zq.at[0, i, pl.ds(0, 7)])
        qt[i, rank_groups[i]] = jnp.sum(zq[0, i], axis=0)
        for _, _, dev in lanes_group[i]:
            send(Q_TILE, i, qt.at[i, rank_groups[i]], qt.at[i, rank_groups[i]], dev)
    for i in range(3):
        arrived(Q_TILE, i, qt.at[i, pl.ds(0, 3)])
        q_now = dot(linv[i], small_right(qt[i].reshape(RANK, 128)), 1, 0)
        qtr[i] = jnp.concatenate(split(q_now, PARTS), axis=0)
        mean_d(i)
        v = fold(dot(qtr[i], mean[i, 0], 1, 1) + dot(qtr[i], mean[i, 1], 1, 1), PARTS)
        slot = slots[i]
        px[i, slot] = pack(v)
        for dev in rows_group[i]:
            send(P_SUM, i, px.at[i, slot], px.at[i, slot], dev)
    for i in range(3):
        arrived(P_SUM, i, px.at[i, pl.ds(0, 7)])
        v = jnp.sum(px[i], axis=0)
        quarter = highs[i] * 2 + c
        pa[i, quarter] = v
        ps = jnp.concatenate(split(unpack(v), PARTS), axis=0)
        v = fold(dot(ps, mean[i, 0], 1, 0) + dot(ps, mean[i, 1], 1, 0), PARTS)
        qx[i] = v.reshape(4, 8, 128)
        qxr[i, rank_groups[i]] = qx[i, rank_groups[i]]
        for yh, cc, dev in lanes_group[i]:
            send(Q_SUM, i, qx.at[i, 2 * cc + yh], qxr.at[i, rank_groups[i]], dev)
    for i in range(3):
        quarter = highs[i] * 2 + c
        for _, _, dev in lanes_group[i]:
            send(P_SHARE, i, pa.at[i, quarter], pa.at[i, quarter], dev)
    for i in range(3):
        arrived(Q_SUM, i, qxr.at[i, pl.ds(0, 3)])
        zq[1, i, z] = jnp.sum(qxr[i], axis=0)
        for dev in column:
            send(Q_Z_2, i, zq.at[1, i, z], zq.at[1, i, z], dev)
    grams = []
    for i in range(3):
        arrived(P_SHARE, i, pa.at[i, pl.ds(0, 3)])
        whole = jnp.concatenate([unpack(pa[i, k]) for k in range(4)], axis=1)
        pw[i] = whole
        grams.append(gram_of(jnp.concatenate(split(whole, PARTS), axis=0)))
    gram_send(GRAM_2, 1, grams)
    for i in range(3):
        arrived(Q_Z_2, i, zq.at[1, i, pl.ds(0, 7)])
        p = ps_index[i]
        qf[i, c, p] = jnp.sum(zq[1, i], axis=0)
        for yy, xx in plane:
            send(Q_GATHER, i, qf.at[i, c, p], qf.at[i, c, p], at(yy, xx))
    factors(GRAM_2, 1)
    for i in range(3):
        p_hat = dot(linv[i], small_right(pw[i]), 1, 0)
        ph, p_low = split(p_hat, 2)
        ps_out[i] = jnp.concatenate([ph, ph, p_low], axis=0)
    for i in range(3):
        arrived(Q_GATHER, i, qf.at[i, 0, pl.ds(0, 15)])
        send(Q_BACK, i, qf.at[i, c], qf.at[i, c], sib)
    for i in range(3):
        arrived(Q_BACK, i, qf.at[i, 0])
        full = qf[i]
        raw = jnp.concatenate(
            [
                jnp.concatenate([full[k // 2, (k % 2) * 8 + l] for l in range(8)], axis=1)
                for k in range(4)
            ],
            axis=0,
        )
        q_now = dot(linv[i], small_right(raw), 1, 0)
        q_out[i] = q_now
        qh, ql = split(q_now, 2)
        qs_out[i] = jnp.concatenate([qh, ql, qh], axis=0)

    sent(P_CORE, pc)
    sent(P_ONE, x1.at[:, :, pl.ds(0, 3)])
    sent(P_TWO, x2.at[:, :, pl.ds(0, 3)])
    sent(P_BACK, pf.at[:, pl.ds(0, 2)])
    sent(GRAM_1, gz.at[0, pl.ds(0, 7)])
    sent(Q_CORE, qc)
    sent(Q_SCATTER, qr.at[:, pl.ds(0, 15)])
    sent(Q_Z_1, zq.at[0, :, pl.ds(0, 7)])
    sent(Q_TILE, qt.at[:, pl.ds(0, 3)])
    sent(M_CORE, wr)
    sent(M_A, ra)
    sent(M_B, rb)
    sent(M_C, rc)
    sent(P_SUM, px.at[:, pl.ds(0, 7)])
    sent(P_SHARE, pa.at[:, pl.ds(0, 3)])
    sent(GRAM_2, gz.at[1, pl.ds(0, 7)])
    sent(Q_SUM, qxr.at[:, pl.ds(0, 3)])
    sent(Q_Z_2, zq.at[1, :, pl.ds(0, 7)])
    sent(Q_GATHER, qf.at[:, 0, pl.ds(0, 15)])
    sent(Q_BACK, qf.at[:, 0])


def exchange(*operands):
    vmem = lambda *shape: pltpu.VMEM(shape, F32)
    scratch = [
        vmem(3, RANK, D),
        pltpu.VMEM((3, PARTS * RANK, D), BF16),
        vmem(3, 4, 8, ROWS),
        vmem(3, 2, 8, ROWS),
        vmem(3, 2, 4, 8, ROWS),
        vmem(3, 2, 4, 8, ROWS),
        vmem(3, 4, 8, ROWS),
        vmem(ITERS, NZ, RANK, 128),
        vmem(3, 2, 2, 8, D),
        vmem(3, 2, 8, D),
        vmem(3, 16, 8, 128),
        vmem(3, 16, 8, 128),
        vmem(ITERS, 3, NZ, 8, 128),
        vmem(3, 4, 8, 128),
        pltpu.VMEM((3, PARTS * RANK, 128), BF16),
        pltpu.VMEM((3, RANK, 6 * RANK), BF16),
        vmem(2, 3, 2, 4, 4, HALF, 128),
        vmem(3, 2, 4, 4, HALF, 128),
        vmem(3, 2, 2, 2, HALF, 128),
        vmem(3, 2, 2, 4, HALF, 128),
        vmem(3, 2, 3, HALF, 128),
        pltpu.VMEM((3, 2, QUART, 128), BF16),
        vmem(3, 8, 24, 128),
        vmem(3, 4, 24, 128),
        vmem(3, RANK, ROWS),
        vmem(3, 4, 8, 128),
        vmem(3, 4, 8, 128),
        vmem(3, 2, 16, 8, 128),
        pltpu.SemaphoreType.DMA((7,)),
        pltpu.SemaphoreType.DMA((20,)),
        pltpu.SemaphoreType.DMA((20, 3)),
        pltpu.SemaphoreType.REGULAR((2,)),
    ]
    inside = pl.BlockSpec(memory_space=pltpu.VMEM)
    outside = pl.BlockSpec(memory_space=pltpu.HBM)
    return pl.pallas_call(
        kernel,
        name="power",
        out_shape=(
            jax.ShapeDtypeStruct((3, RANK, D), F32),
            jax.ShapeDtypeStruct((3, 3 * RANK, ROWS), BF16),
            jax.ShapeDtypeStruct((3, 3 * RANK, D), BF16),
            jax.ShapeDtypeStruct((2, ROWS, D), BF16),
            jax.ShapeDtypeStruct((2, ROWS, D), BF16),
            jax.ShapeDtypeStruct((D, ROWS), BF16),
            jax.ShapeDtypeStruct((D, ROWS), BF16),
        ),
        in_specs=[outside] * 7,
        out_specs=(inside,) * 7,
        scratch_shapes=scratch,
        compiler_params=pltpu.CompilerParams(
            collective_id=0, has_side_effects=True, vmem_limit_bytes=32 << 20
        ),
        cost_estimate=pl.CostEstimate(flops=10**9, bytes_accessed=6 * 10**6, transcendentals=0),
    )(*operands)


PIECES = 4
TALL = ROWS // PIECES
FLAT = D // PIECES


def finish_kernel(ps, qs, q, gm, em, gd, ed, u0, u1, u2, n0, n1, n2, q_out, um, nm, ud, nd, sem):
    copies = []

    def out(src, dst):
        cp = pltpu.make_async_copy(src, dst, sem.at[len(copies)])
        cp.start()
        copies.append(cp)

    out(q, q_out)
    for i, (u, n) in enumerate(((u0, n0), (u1, n1))):
        for k in range(PIECES):
            rows = pl.ds(k * TALL, TALL)
            v = dot(ps[i, :, k * TALL : (k + 1) * TALL], qs[i], 0, 0)
            um[i, rows] = v.astype(BF16)
            nm[i, rows] = ((gm[i, rows].astype(F32) + em[i, rows].astype(F32)) - v).astype(BF16)
            out(um.at[i, rows], u.at[rows])
            out(nm.at[i, rows], n.at[rows])
    for k in range(PIECES):
        rows = pl.ds(k * FLAT, FLAT)
        v = dot(qs[2, :, k * FLAT : (k + 1) * FLAT], ps[2], 0, 0)
        ud[rows] = v.astype(BF16)
        nd[rows] = ((gd[rows].astype(F32) + ed[rows].astype(F32)) - v).astype(BF16)
        out(ud.at[rows], u2.at[rows])
        out(nd.at[rows], n2.at[rows])
    for cp in copies:
        cp.wait()


def finish(ps, qs, q, gm, em, gd, ed):
    inside = pl.BlockSpec(memory_space=pltpu.VMEM)
    outside = pl.BlockSpec(memory_space=pltpu.HBM)
    shapes = [(ROWS, D), (ROWS, D), (D, ROWS)]
    outs = [jax.ShapeDtypeStruct(shape, BF16) for shape in shapes]
    return pl.pallas_call(
        finish_kernel,
        name="finish",
        in_specs=[inside] * 7,
        out_specs=[outside] * 7,
        out_shape=outs + outs + [jax.ShapeDtypeStruct((3, RANK, D), F32)],
        scratch_shapes=[
            pltpu.VMEM((2, ROWS, D), BF16),
            pltpu.VMEM((2, ROWS, D), BF16),
            pltpu.VMEM((D, ROWS), BF16),
            pltpu.VMEM((D, ROWS), BF16),
            pltpu.SemaphoreType.DMA((6 * PIECES + 1,)),
        ],
        compiler_params=pltpu.CompilerParams(vmem_limit_bytes=24 << 20),
    )(ps, qs, q, gm, em, gd, ed)


def shards(gate_grad, up_grad, down_grad, gate_error, up_error, down_error, q_init):
    grads = (gate_grad[0], up_grad[0], down_grad[0])
    errors = (gate_error[0], up_error[0], down_error[0])
    pinned = [
        pltpu.with_memory_space_constraint(v, pltpu.HBM)
        for v in grads + errors + (jnp.swapaxes(q_init, 1, 2),)
    ]
    q, ps, qs, *held = exchange(*pinned)
    u0, u1, u2, n0, n1, n2, q_next = finish(ps, qs, q, *held)
    return u0, u1, u2, n0[None], n1[None], n2[None], jnp.swapaxes(q_next, 1, 2)


def solution(mesh):
    in_specs = (
        P("replica", "tensor", None),
        P("replica", "tensor", None),
        P("replica", None, "tensor"),
        P("replica", "tensor", None),
        P("replica", "tensor", None),
        P("replica", None, "tensor"),
        P(),
    )
    out_specs = (
        P("tensor", None),
        P("tensor", None),
        P(None, "tensor"),
        P("replica", "tensor", None),
        P("replica", "tensor", None),
        P("replica", None, "tensor"),
        P(),
    )
    return jax.shard_map(shards, mesh=mesh, in_specs=in_specs, out_specs=out_specs, check_vma=False)
```

```python
import jax
import jax.numpy as jnp
from jax import lax
from jax.experimental import pallas as pl
from jax.experimental.pallas import tpu as pltpu
from jax.sharding import PartitionSpec as P

ITERS = 2
D = 1024
RANK = 32
ROWS = 384
NY, NX, NZ = 4, 4, 8
MESH = pl.DeviceIdType.MESH
F32 = jnp.float32
BF16 = jnp.bfloat16
PARTS = 2

(
    P_CORE, P_ONE, P_TWO, P_BACK, GRAM_1, Q_CORE, Q_SCATTER, Q_Z_1, Q_TILE,
    M_CORE, M_A, M_B, M_C,
    P_SUM, P_SHARE, GRAM_2, Q_SUM, Q_Z_2, Q_GATHER, Q_BACK,
) = range(20)
QUART = 96
HALF = 48


def split(x, parts):
    out = []
    for k in range(parts):
        piece = x.astype(BF16)
        out.append(piece)
        if k + 1 < parts:
            x = x - piece.astype(F32)
    return out


def dot(a, b, ca, cb):
    return lax.dot_general(a, b, (((ca,), (cb,)), ((), ())), preferred_element_type=F32)


def small_left(a, cat_axis):
    h, m, l = split(a, 3)
    return jnp.concatenate([h, h, m, h, l, m], axis=cat_axis)


def small_right(b):
    h, m, l = split(b, 3)
    return jnp.concatenate([h, m, h, l, h, m], axis=0)


def pack(v):
    tail = jnp.concatenate([v[24:, k * 32 : (k + 1) * 32] for k in range(3)], axis=0)
    return jnp.concatenate([v[:24], tail], axis=1)


def unpack(v):
    tail = jnp.concatenate([v[8 * k : 8 * k + 8, QUART:] for k in range(3)], axis=1)
    return jnp.concatenate([v[:, :QUART], tail], axis=0)


def fold(x, parts):
    total = x[(parts - 1) * RANK :]
    for k in range(parts - 2, -1, -1):
        total = total + x[k * RANK : (k + 1) * RANK]
    return total


def inverse_factors(grams):
    row = lax.broadcasted_iota(jnp.int32, (RANK, 2 * RANK), 0)
    lane = lax.broadcasted_iota(jnp.int32, (RANK, 2 * RANK), 1)
    eye = (lane == row + RANK).astype(F32)
    augs = []
    for g in grams:
        augs.append(jnp.concatenate([g, jnp.zeros_like(g)], axis=1) + eye)
    for j in range(RANK):
        for n in range(len(augs)):
            a = augs[n]
            pivot = a[j : j + 1, j : j + 1]
            r = lax.rsqrt(pivot)
            r = r * (1.5 - 0.5 * pivot * r * r)
            top = a[j : j + 1, :] * r
            col = a[:, j : j + 1] * r
            a = jnp.where(row > j, a - col * top, jnp.where(row == j, top, a))
            augs[n] = a
    return [a[:, RANK:] for a in augs]


def kernel(
    g0, g1, g2, e0, e1, e2, q0,
    q_out, ps_out, qs_out, mm, md,
    gm, em, gd, ed, qi, qs, pt, pc, x1, x2, pf, gz, qp, qc, qsum, qr, zq, qt, qtr, linv,
    wb, wr, ra, rb, rc, mean, px, pa, pw, qx, qxr, qf,
    load, ssem, rsem, know,
):
    r = lax.axis_index("replica")
    z = lax.axis_index("tensor")
    y, x, c = r // 8, (r // 2) % 4, r % 2
    ps_index = (y * 4 + x, x * 4 + y, y * 4 + x)
    other = 1 - c
    sib = (y * 8 + x * 2 + other, z)

    def at(yy, xx):
        return (yy * 8 + xx * 2 + c, z)

    plane = [
        ((y + dy) % NY, (x + dx) % NX)
        for dy, dx in [
            (2, 2), (2, 1), (1, 2), (2, 3), (3, 2), (1, 1), (1, 3), (3, 1), (3, 3),
            (2, 0), (0, 2), (1, 0), (0, 1), (3, 0), (0, 3),
        ]
    ]
    column = [(r, (z + dz) % NZ) for dz in (4, 3, 5, 2, 6, 1, 7)]
    xs = [at(y, (x + d) % NX) for d in (2, 1, 3)]
    ys = [at((y + d) % NY, x) for d in (2, 1, 3)]
    yflip, xflip = (y // 2) * 2 + (1 - y % 2), (x // 2) * 2 + (1 - x % 2)
    along_x = [at(yflip, (x + d) % NX) for d in (2, 1, 3, 0)] + xs
    along_y = [at((y + d) % NY, xflip) for d in (2, 1, 3, 0)] + ys
    rows_group = (along_x, along_y, along_x)
    yopp, xopp = (y + 2) % NY, (x + 2) % NX

    def four(high, yy, xx):
        return [
            (1 - high, other, (yy * 8 + xx * 2 + other, z)),
            (1 - high, c, at(yy, xx)),
            (high, other, sib),
        ]

    lanes_group = (four(y // 2, yopp, x), four(x // 2, y, xopp), four(y // 2, yopp, x))
    highs, slots = (y // 2, x // 2, y // 2), ((y % 2) * 4 + x, (x % 2) * 4 + y, (y % 2) * 4 + x)
    rank_groups = [2 * c + high for high in highs]

    barrier = pltpu.get_barrier_semaphore()
    near = [(r, (z + dz) % NZ) for dz in (1, 7)]
    next_near = [(r, (z + dz) % NZ) for dz in (2, 6)]
    greet = xs + ys + near + [sib]
    for dev in greet:
        pl.semaphore_signal(barrier, inc=1, device_id=dev, device_id_type=MESH)

    loads = []
    for i, (src, dst) in enumerate(
        [(g0, gm.at[0]), (e0, em.at[0]), (g1, gm.at[1]), (e1, em.at[1]), (g2, gd), (e2, ed), (q0, qi)]
    ):
        cp = pltpu.make_async_copy(src, dst, load.at[i])
        loads.append(cp)
    for k in (6, 0, 1, 2, 3, 4, 5):
        loads[k].start()

    def send(stage, i, src, dst, dev):
        pltpu.make_async_remote_copy(
            src_ref=src,
            dst_ref=dst,
            send_sem=ssem.at[stage],
            recv_sem=rsem.at[stage, i],
            device_id=dev,
            device_id_type=MESH,
        ).start()

    def arrived(stage, i, like):
        pltpu.make_async_copy(like, like, rsem.at[stage, i]).wait()

    def sent(stage, like):
        pltpu.make_async_copy(like, like, ssem.at[stage]).wait()

    def tell(k, devs):
        for dev in devs:
            pl.semaphore_signal(know.at[k], inc=1, device_id=dev, device_id_type=MESH)

    place = ((x, y), (y, x))
    step = ((xs[1], xs[2]), (ys[1], ys[2]))
    own = wb.at[c]

    def mean_core(i):
        def put(rows_from, lanes_from, v):
            quarter, h = rows_from // QUART, (rows_from // HALF) % 2
            for k in range(v.shape[1] // 128):
                tile = lanes_from // 128 + k
                ty, tx = (quarter // 2) * 2 + tile // 4, tile % 4
                a, b = (tx, ty) if (h == 0) == (i != 1) else (ty, tx)
                wb[quarter % 2, i, h, a, b] = v[:, k * 128 : (k + 1) * 128]

        if i == 2:
            for tile in range(8):
                f = slice(tile * 128, (tile + 1) * 128)
                v = gd[f].astype(F32) + ed[f].astype(F32)
                md[f] = v
                v = (v * (1.0 / 32.0)).T
                for k in range(8):
                    put(k * HALF, tile * 128, v[k * HALF : (k + 1) * HALF])
        else:
            for k in range(8):
                f = slice(k * HALF, (k + 1) * HALF)
                v = gm[i, f].astype(F32) + em[i, f].astype(F32)
                mm[i, f] = v
                put(k * HALF, 0, v * (1.0 / 32.0))
        send(M_CORE, i, wb.at[other, i], wr.at[i], sib)

    def mean_a(i):
        arrived(M_CORE, i, wr.at[i])
        wb[c, i] = wb[c, i] + wr[i]
        for h in range(2):
            a, _ = place[h]
            plus, minus = step[h]
            send(M_A, i, own.at[i, h, (a + 2) % 4, pl.ds(0, 2)], ra.at[i, h, 0], plus)
            send(M_A, i, own.at[i, h, (a + 2) % 4, pl.ds(2, 2)], ra.at[i, h, 1], minus)

    def mean_b(i):
        arrived(M_A, i, ra.at[i])
        for h in range(2):
            a, _ = place[h]
            up, down = (a + 1) % 4, (a + 3) % 4
            plus, minus = step[h]
            wb[c, i, h, up, pl.ds(0, 2)] = wb[c, i, h, up, pl.ds(0, 2)] + ra[i, h, 0]
            wb[c, i, h, down, pl.ds(2, 2)] = wb[c, i, h, down, pl.ds(2, 2)] + ra[i, h, 1]
            send(M_B, i, own.at[i, h, up], rb.at[i, h, 0], plus)
            send(M_B, i, own.at[i, h, down], rb.at[i, h, 1], minus)

    def mean_c(i):
        arrived(M_B, i, rb.at[i])
        for h in range(2):
            a, b = place[h]
            wb[c, i, h, a] = wb[c, i, h, a] + rb[i, h, 0] + rb[i, h, 1]
            for k in range(3):
                d = (2, 1, 3)[k]
                dev = (ys, xs)[h][k]
                send(M_C, i, own.at[i, h, a, (b + d) % 4], rc.at[i, h, k], dev)

    def mean_d(i):
        arrived(M_C, i, rc.at[i])
        for h in range(2):
            a, b = place[h]
            v = wb[c, i, h, a, b] + rc[i, h, 0] + (rc[i, h, 1] + rc[i, h, 2])
            hi, lo = split(v, 2)
            mean[i, 0, h * HALF : (h + 1) * HALF] = hi
            mean[i, 1, h * HALF : (h + 1) * HALF] = lo

    loads[6].wait()
    for i in range(3):
        qs[i] = jnp.concatenate(split(qi[i], PARTS), axis=0)

    def project(i):
        if i == 2:
            v = dot(qs[i], gd[...], 1, 0) + dot(qs[i], ed[...], 1, 0)
        else:
            v = dot(qs[i], gm[i], 1, 1) + dot(qs[i], em[i], 1, 1)
        return fold(v, PARTS) * (1.0 / 32.0)

    def back_project(i, ps):
        if i == 2:
            v = dot(ps, gd[...], 1, 1) + dot(ps, ed[...], 1, 1)
        else:
            v = dot(ps, gm[i], 1, 0) + dot(ps, em[i], 1, 0)
        return fold(v, PARTS) * (1.0 / 32.0)

    def gram_of(ps):
        gg = fold(dot(ps, ps, 1, 1), PARTS)
        gram = gg[:, (PARTS - 1) * RANK :]
        for k in range(PARTS - 2, -1, -1):
            gram = gram + gg[:, k * RANK : (k + 1) * RANK]
        return gram

    def gram_send(stage, t, grams):
        gz[t, z] = jnp.concatenate(grams + [jnp.zeros((RANK, RANK), F32)], axis=1)
        for dev in column:
            send(stage, 0, gz.at[t, z], gz.at[t, z], dev)

    def factors(stage, t):
        arrived(stage, 0, gz.at[t, pl.ds(0, 7)])
        gram = jnp.sum(gz[t], axis=0)
        inv = inverse_factors([gram[:, k * RANK : (k + 1) * RANK] for k in range(3)])
        for i in range(3):
            linv[i] = small_left(inv[i], 1)

    for i in range(3):
        loads[2 * i].wait()
        loads[2 * i + 1].wait()
        pt[i] = project(i).reshape(4, 8, ROWS)
        if i == 0:
            pl.semaphore_wait(barrier, len(greet))
        send(P_CORE, i, pt.at[i, pl.ds(2 * other, 2)], pc.at[i], sib)
    tell(0, near)
    mean_core(0)
    for i in range(3):
        arrived(P_CORE, i, pc.at[i])
        s = pt[i, pl.ds(2 * c, 2)] + pc[i]
        x1[i, 0, x] = s[0]
        x1[i, 1, y] = s[1]
        for dev in xs:
            send(P_ONE, i, x1.at[i, 0, x], x1.at[i, 0, x], dev)
        for dev in ys:
            send(P_ONE, i, x1.at[i, 1, y], x1.at[i, 1, y], dev)
    mean_core(1)
    mean_core(2)
    mean_a(0)
    for i in range(3):
        arrived(P_ONE, i, x1.at[i, :, pl.ds(0, 3)])
        a = (x1[i, 0, 0] + x1[i, 0, 1]) + (x1[i, 0, 2] + x1[i, 0, 3])
        b = (x1[i, 1, 0] + x1[i, 1, 1]) + (x1[i, 1, 2] + x1[i, 1, 3])
        x2[i, 0, y] = a
        x2[i, 1, x] = b
        for dev in ys:
            send(P_TWO, i, x2.at[i, 0, y], x2.at[i, 0, y], dev)
        for dev in xs:
            send(P_TWO, i, x2.at[i, 1, x], x2.at[i, 1, x], dev)
    pl.semaphore_wait(know.at[0], 2)
    tell(1, next_near)
    mean_a(1)
    mean_a(2)
    mean_b(0)
    for i in range(3):
        arrived(P_TWO, i, x2.at[i, :, pl.ds(0, 3)])
        a = (x2[i, 0, 0] + x2[i, 0, 1]) + (x2[i, 0, 2] + x2[i, 0, 3])
        b = (x2[i, 1, 0] + x2[i, 1, 1]) + (x2[i, 1, 2] + x2[i, 1, 3])
        pf[i, 2 * c] = a
        pf[i, 2 * c + 1] = b
        send(P_BACK, i, pf.at[i, pl.ds(2 * c, 2)], pf.at[i, pl.ds(2 * c, 2)], sib)
    pl.semaphore_wait(know.at[1], 2)
    grams = []
    for i in range(3):
        arrived(P_BACK, i, pf.at[i, pl.ds(0, 2)])
        ps = jnp.concatenate(split(pf[i].reshape(RANK, ROWS), PARTS), axis=0)
        qp[i] = back_project(i, ps).reshape(2, 2, 8, D)
        send(Q_CORE, i, qp.at[i, other], qc.at[i], sib)
        grams.append(gram_of(ps))
    gram_send(GRAM_1, 0, grams)
    for i in range(3):
        arrived(Q_CORE, i, qc.at[i])
        s = qp[i, c] + qc[i]
        for k in range(16):
            qsum[i, k] = s[k // 8, :, (k % 8) * 128 : (k % 8 + 1) * 128]
        p = ps_index[i]
        qr[i, p] = qsum[i, p]
        for yy, xx in plane:
            there = xx * 4 + yy if i == 1 else yy * 4 + xx
            send(Q_SCATTER, i, qsum.at[i, there], qr.at[i, p], at(yy, xx))
    mean_b(1)
    mean_b(2)
    for i in range(3):
        arrived(Q_SCATTER, i, qr.at[i, pl.ds(0, 15)])
        zq[0, i, z] = jnp.sum(qr[i], axis=0)
        for dev in column:
            send(Q_Z_1, i, zq.at[0, i, z], zq.at[0, i, z], dev)
    mean_c(0)
    factors(GRAM_1, 0)
    for i in range(1, 3):
        mean_c(i)
    for i in range(3):
        arrived(Q_Z_1, i, zq.at[0, i, pl.ds(0, 7)])
        qt[i, rank_groups[i]] = jnp.sum(zq[0, i], axis=0)
        for _, _, dev in lanes_group[i]:
            send(Q_TILE, i, qt.at[i, rank_groups[i]], qt.at[i, rank_groups[i]], dev)
    for i in range(3):
        arrived(Q_TILE, i, qt.at[i, pl.ds(0, 3)])
        q_now = dot(linv[i], small_right(qt[i].reshape(RANK, 128)), 1, 0)
        qtr[i] = jnp.concatenate(split(q_now, PARTS), axis=0)
        mean_d(i)
        v = fold(dot(qtr[i], mean[i, 0], 1, 1) + dot(qtr[i], mean[i, 1], 1, 1), PARTS)
        slot = slots[i]
        px[i, slot] = pack(v)
        for dev in rows_group[i]:
            send(P_SUM, i, px.at[i, slot], px.at[i, slot], dev)
    for i in range(3):
        arrived(P_SUM, i, px.at[i, pl.ds(0, 7)])
        v = jnp.sum(px[i], axis=0)
        quarter = highs[i] * 2 + c
        pa[i, quarter] = v
        ps = jnp.concatenate(split(unpack(v), PARTS), axis=0)
        v = fold(dot(ps, mean[i, 0], 1, 0) + dot(ps, mean[i, 1], 1, 0), PARTS)
        qx[i] = v.reshape(4, 8, 128)
        qxr[i, rank_groups[i]] = qx[i, rank_groups[i]]
        for yh, cc, dev in lanes_group[i]:
            send(Q_SUM, i, qx.at[i, 2 * cc + yh], qxr.at[i, rank_groups[i]], dev)
    for i in range(3):
        quarter = highs[i] * 2 + c
        for _, _, dev in lanes_group[i]:
            send(P_SHARE, i, pa.at[i, quarter], pa.at[i, quarter], dev)
    for i in range(3):
        arrived(Q_SUM, i, qxr.at[i, pl.ds(0, 3)])
        zq[1, i, z] = jnp.sum(qxr[i], axis=0)
        for dev in column:
            send(Q_Z_2, i, zq.at[1, i, z], zq.at[1, i, z], dev)
    grams = []
    for i in range(3):
        arrived(P_SHARE, i, pa.at[i, pl.ds(0, 3)])
        whole = jnp.concatenate([unpack(pa[i, k]) for k in range(4)], axis=1)
        pw[i] = whole
        grams.append(gram_of(jnp.concatenate(split(whole, PARTS), axis=0)))
    gram_send(GRAM_2, 1, grams)
    for i in range(3):
        arrived(Q_Z_2, i, zq.at[1, i, pl.ds(0, 7)])
        p = ps_index[i]
        qf[i, c, p] = jnp.sum(zq[1, i], axis=0)
        for yy, xx in plane:
            send(Q_GATHER, i, qf.at[i, c, p], qf.at[i, c, p], at(yy, xx))
    factors(GRAM_2, 1)
    for i in range(3):
        arrived(Q_GATHER, i, qf.at[i, 0, pl.ds(0, 15)])
        send(Q_BACK, i, qf.at[i, c], qf.at[i, c], sib)
    for i in range(3):
        p_hat = dot(linv[i], small_right(pw[i]), 1, 0)
        ph, p_low = split(p_hat, 2)
        ps_out[i] = jnp.concatenate([ph, ph, p_low], axis=0)
    for i in range(3):
        arrived(Q_BACK, i, qf.at[i, 0])
        full = qf[i]
        raw = jnp.concatenate(
            [
                jnp.concatenate([full[k // 2, (k % 2) * 8 + l] for l in range(8)], axis=1)
                for k in range(4)
            ],
            axis=0,
        )
        q_now = dot(linv[i], small_right(raw), 1, 0)
        q_out[i] = q_now
        qh, ql = split(q_now, 2)
        qs_out[i] = jnp.concatenate([qh, ql, qh], axis=0)

    sent(P_CORE, pc)
    sent(P_ONE, x1.at[:, :, pl.ds(0, 3)])
    sent(P_TWO, x2.at[:, :, pl.ds(0, 3)])
    sent(P_BACK, pf.at[:, pl.ds(0, 2)])
    sent(GRAM_1, gz.at[0, pl.ds(0, 7)])
    sent(Q_CORE, qc)
    sent(Q_SCATTER, qr.at[:, pl.ds(0, 15)])
    sent(Q_Z_1, zq.at[0, :, pl.ds(0, 7)])
    sent(Q_TILE, qt.at[:, pl.ds(0, 3)])
    sent(M_CORE, wr)
    sent(M_A, ra)
    sent(M_B, rb)
    sent(M_C, rc)
    sent(P_SUM, px.at[:, pl.ds(0, 7)])
    sent(P_SHARE, pa.at[:, pl.ds(0, 3)])
    sent(GRAM_2, gz.at[1, pl.ds(0, 7)])
    sent(Q_SUM, qxr.at[:, pl.ds(0, 3)])
    sent(Q_Z_2, zq.at[1, :, pl.ds(0, 7)])
    sent(Q_GATHER, qf.at[:, 0, pl.ds(0, 15)])
    sent(Q_BACK, qf.at[:, 0])


def exchange(*operands):
    vmem = lambda *shape: pltpu.VMEM(shape, F32)
    scratch = [
        pltpu.VMEM((2, ROWS, D), BF16),
        pltpu.VMEM((2, ROWS, D), BF16),
        pltpu.VMEM((D, ROWS), BF16),
        pltpu.VMEM((D, ROWS), BF16),
        vmem(3, RANK, D),
        pltpu.VMEM((3, PARTS * RANK, D), BF16),
        vmem(3, 4, 8, ROWS),
        vmem(3, 2, 8, ROWS),
        vmem(3, 2, 4, 8, ROWS),
        vmem(3, 2, 4, 8, ROWS),
        vmem(3, 4, 8, ROWS),
        vmem(ITERS, NZ, RANK, 128),
        vmem(3, 2, 2, 8, D),
        vmem(3, 2, 8, D),
        vmem(3, 16, 8, 128),
        vmem(3, 16, 8, 128),
        vmem(ITERS, 3, NZ, 8, 128),
        vmem(3, 4, 8, 128),
        pltpu.VMEM((3, PARTS * RANK, 128), BF16),
        pltpu.VMEM((3, RANK, 6 * RANK), BF16),
        vmem(2, 3, 2, 4, 4, HALF, 128),
        vmem(3, 2, 4, 4, HALF, 128),
        vmem(3, 2, 2, 2, HALF, 128),
        vmem(3, 2, 2, 4, HALF, 128),
        vmem(3, 2, 3, HALF, 128),
        pltpu.VMEM((3, 2, QUART, 128), BF16),
        vmem(3, 8, 24, 128),
        vmem(3, 4, 24, 128),
        vmem(3, RANK, ROWS),
        vmem(3, 4, 8, 128),
        vmem(3, 4, 8, 128),
        vmem(3, 2, 16, 8, 128),
        pltpu.SemaphoreType.DMA((7,)),
        pltpu.SemaphoreType.DMA((20,)),
        pltpu.SemaphoreType.DMA((20, 3)),
        pltpu.SemaphoreType.REGULAR((2,)),
    ]
    inside = pl.BlockSpec(memory_space=pltpu.VMEM)
    outside = pl.BlockSpec(memory_space=pltpu.HBM)
    return pl.pallas_call(
        kernel,
        name="power",
        out_shape=(
            jax.ShapeDtypeStruct((3, RANK, D), F32),
            jax.ShapeDtypeStruct((3, 3 * RANK, ROWS), BF16),
            jax.ShapeDtypeStruct((3, 3 * RANK, D), BF16),
            jax.ShapeDtypeStruct((2, ROWS, D), F32),
            jax.ShapeDtypeStruct((D, ROWS), F32),
        ),
        in_specs=[outside] * 7,
        out_specs=(inside,) * 5,
        scratch_shapes=scratch,
        compiler_params=pltpu.CompilerParams(
            collective_id=0, has_side_effects=True, vmem_limit_bytes=32 << 20
        ),
        cost_estimate=pl.CostEstimate(flops=10**9, bytes_accessed=6 * 10**6, transcendentals=0),
    )(*operands)


PIECES = 4
TALL = ROWS // PIECES
FLAT = D // PIECES


def finish_kernel(ps, qs, q, mm, md, u0, u1, u2, n0, n1, n2, q_out, um, nm, ud, nd, sem):
    copies = []

    def out(src, dst):
        cp = pltpu.make_async_copy(src, dst, sem.at[len(copies)])
        cp.start()
        copies.append(cp)

    out(q, q_out)
    for i, (u, n) in enumerate(((u0, n0), (u1, n1))):
        for k in range(PIECES):
            rows = pl.ds(k * TALL, TALL)
            v = dot(ps[i, :, k * TALL : (k + 1) * TALL], qs[i], 0, 0)
            um[i, rows] = v.astype(BF16)
            nm[i, rows] = (mm[i, rows] - v).astype(BF16)
            out(um.at[i, rows], u.at[rows])
            out(nm.at[i, rows], n.at[rows])
    for k in range(PIECES):
        rows = pl.ds(k * FLAT, FLAT)
        v = dot(qs[2, :, k * FLAT : (k + 1) * FLAT], ps[2], 0, 0)
        ud[rows] = v.astype(BF16)
        nd[rows] = (md[rows] - v).astype(BF16)
        out(ud.at[rows], u2.at[rows])
        out(nd.at[rows], n2.at[rows])
    for cp in copies:
        cp.wait()


def finish(ps, qs, q, mm, md):
    inside = pl.BlockSpec(memory_space=pltpu.VMEM)
    outside = pl.BlockSpec(memory_space=pltpu.HBM)
    shapes = [(ROWS, D), (ROWS, D), (D, ROWS)]
    outs = [jax.ShapeDtypeStruct(shape, BF16) for shape in shapes]
    return pl.pallas_call(
        finish_kernel,
        name="finish",
        in_specs=[inside] * 5,
        out_specs=[outside] * 7,
        out_shape=outs + outs + [jax.ShapeDtypeStruct((3, RANK, D), F32)],
        scratch_shapes=[
            pltpu.VMEM((2, ROWS, D), BF16),
            pltpu.VMEM((2, ROWS, D), BF16),
            pltpu.VMEM((D, ROWS), BF16),
            pltpu.VMEM((D, ROWS), BF16),
            pltpu.SemaphoreType.DMA((6 * PIECES + 1,)),
        ],
        compiler_params=pltpu.CompilerParams(vmem_limit_bytes=24 << 20),
    )(ps, qs, q, mm, md)


def shards(gate_grad, up_grad, down_grad, gate_error, up_error, down_error, q_init):
    grads = (gate_grad[0], up_grad[0], down_grad[0])
    errors = (gate_error[0], up_error[0], down_error[0])
    pinned = [
        pltpu.with_memory_space_constraint(v, pltpu.HBM)
        for v in grads + errors + (jnp.swapaxes(q_init, 1, 2),)
    ]
    q, ps, qs, *held = exchange(*pinned)
    u0, u1, u2, n0, n1, n2, q_next = finish(ps, qs, q, *held)
    return u0, u1, u2, n0[None], n1[None], n2[None], jnp.swapaxes(q_next, 1, 2)


def solution(mesh):
    in_specs = (
        P("replica", "tensor", None),
        P("replica", "tensor", None),
        P("replica", None, "tensor"),
        P("replica", "tensor", None),
        P("replica", "tensor", None),
        P("replica", None, "tensor"),
        P(),
    )
    out_specs = (
        P("tensor", None),
        P("tensor", None),
        P(None, "tensor"),
        P("replica", "tensor", None),
        P("replica", "tensor", None),
        P("replica", None, "tensor"),
        P(),
    )
    return jax.shard_map(shards, mesh=mesh, in_specs=in_specs, out_specs=out_specs, check_vma=False)
```
